256 devices in a mesh: blk: 8 (over y, x_lo), fsdp: 32 (over x_hi, z, core).
Axes of the slice: x: 4 (x_hi: 2, x_lo: 2; x = x_hi * 2 + x_lo), y: 4, z: 8, core: 2. Of those that a mesh axis runs over, the one named last changes fastest.
Arguments:
- hidden: bfloat16 [131072, 8192], P(('blk', 'fsdp')), may hold values from -24 to 24
- gain: bfloat16 [8, 8192], P('blk', 'fsdp'), may hold values from 0.099609375 to 1.8984375
- value_weight: bfloat16 [8, 8192, 512], P('blk', 'fsdp'), may hold values from -0.0625 to 0.0625
- cotangent: bfloat16 [131072, 512], P(('blk', 'fsdp')), may hold values from -0.059814453 to 0.059814453
- grad_weight_in: float32 [8, 8192, 512], P('blk', 'fsdp'), may hold values from -6 to 6
- grad_gain_in: float32 [8, 8192], P('blk', 'fsdp'), may hold values from -1.8 to 1.8
Outputs:
- values: bfloat16 [131072, 512], P(('blk', 'fsdp'))
- grad_weight: float32 [8, 8192, 512], P('blk', 'fsdp')
- grad_gain: float32 [8, 8192], P('blk', 'fsdp')
The draws below stay inside these ranges and needn't reach their ends.
All inputs are finite; a program needn't handle non-finite values.
Results may differ from the reference program's by a relative error of at most 0.018.
Values may be sent and summed in bfloat16 or wider, within the bound.
No kernel may reach another device: no remote copies, remote signals or barrier semaphores. Data moves between devices by JAX's collectives and lax.ppermute only.
A program may use at most 128 MiB of HBM per device.

```python
import jax
import jax.numpy as jnp
from jax import lax

D = 8192
V = 512
TOK_DEV = 512
LAYERS = 8
TOKENS = 131072
N_BLK = 8
N_FSDP = 32


def raised(entries, own_key, source, target, shards_of, factor):
    def block_of(axis_at):
        return (jnp.arange(entries.shape[axis_at]) // (entries.shape[axis_at] // shards_of)).reshape((-1,) + (1,) * (entries.ndim - 1 - axis_at))

    one_side = jax.random.permutation(own_key, shards_of)[block_of(target)]
    other_side = (block_of(target) + shards_of // 2) % shards_of
    return jnp.where((block_of(source) == one_side) | (block_of(source) == other_side), factor * entries, entries)


def levels(stream_key, shape, pieces, low, largest):
    factor_of = 1.0
    for dim, parts in pieces:
        heights = jax.random.uniform(jax.random.fold_in(jax.random.fold_in(stream_key, 6), dim), (parts,), jnp.float32, low / len(pieces), largest / len(pieces))
        factor_of = factor_of * jnp.repeat(jnp.exp(heights), shape[dim] // parts).reshape((-1,) + (1,) * (len(shape) - 1 - dim))
    return factor_of


def gaussian(key, dims, width, bound, split=(), dtype=jnp.bfloat16):
    factor_of = levels(key, dims, split, -0.22, 0.18) if split else 1.0
    result = jax.random.normal(key, dims, jnp.float32) * width * factor_of
    return jnp.minimum(jnp.maximum(result, -bound), bound).astype(dtype)


def heavy_noise(rng, dims, deviation, reach, cuts, heavy, held_as=jnp.bfloat16):
    values = deviation * jax.random.normal(rng, dims, jnp.float32)
    if cuts:
        values = values * levels(rng, dims, cuts, -0.22, 0.18)
    return jnp.clip(raised(values, jax.random.fold_in(rng, 3), *heavy), -reach, reach).astype(held_as)


def setup_inputs(seed: int = 0) -> dict:
    keys = jax.random.split(jax.random.key(seed), 7)
    hidden = heavy_noise(keys[0], (TOKENS, D), 1.0, 24.0, ((0, 256),), (0, 1, 256, 6.0))
    gain = jnp.clip(1.0 + 0.18 * jax.random.normal(keys[1], (LAYERS, D), jnp.float32), 0.099609375, 1.8984375).astype(jnp.bfloat16)
    value_weight = gaussian(keys[2], (LAYERS, D, V), D ** -0.5, 0.0625, ((0, 8), (1, 32)))
    cotangent = gaussian(keys[3], (TOKENS, V), 0.01, 0.059814453, ((0, 256),))
    grad_weight_in = gaussian(keys[4], (LAYERS, D, V), 1.0, 6.0, ((0, 8), (1, 32)), jnp.float32)
    grad_gain_in = gaussian(keys[5], (LAYERS, D), 0.3, 1.8, ((0, 8), (1, 32)), jnp.float32)
    return {"hidden": hidden, "gain": gain, "value_weight": value_weight, "cotangent": cotangent, "grad_weight_in": grad_weight_in, "grad_gain_in": grad_gain_in}


def add_device(total, pair):
    scaled_rows, cot_rows = pair
    term = jnp.dot(scaled_rows.T, cot_rows, preferred_element_type=jnp.float32).astype(jnp.bfloat16)
    term = lax.optimization_barrier(term)
    return (total + term.astype(jnp.float32), None)

def reference(hidden, gain, value_weight, cotangent, grad_weight_in, grad_gain_in):
    micro = TOK_DEV * N_FSDP
    value_list = []
    weight_parts = {}
    gain_parts = {}
    for block in range(N_BLK):
        layer = (block - 1) % N_BLK
        rows = hidden[block * micro:(block + 1) * micro].astype(jnp.float32)
        normed = rows * lax.rsqrt(lax.optimization_barrier(jnp.mean(rows * rows, axis=-1, keepdims=True)) + 1e-05)
        scaled = (normed * gain[layer].astype(jnp.float32)).astype(jnp.bfloat16)
        value_list.append(jnp.dot(scaled, value_weight[layer], preferred_element_type=jnp.float32).astype(jnp.bfloat16))
        cot = cotangent[block * micro:(block + 1) * micro]
        back = jnp.dot(cot, value_weight[layer].T, preferred_element_type=jnp.float32)
        gain_parts[layer] = lax.optimization_barrier(jnp.sum(back * normed, axis=0))
        pairs = (scaled.reshape(N_FSDP, TOK_DEV, D), cot.reshape(N_FSDP, TOK_DEV, V))
        total, _ = lax.scan(add_device, jnp.zeros((D, V), jnp.float32), pairs)
        weight_parts[layer] = total
    values = jnp.concatenate(value_list, axis=0)
    grad_weight = jnp.stack([grad_weight_in[layer] + weight_parts[layer] for layer in range(N_BLK)])
    grad_gain = jnp.stack([grad_gain_in[layer] + gain_parts[layer] for layer in range(N_BLK)])
    return (values, grad_weight, grad_gain)
```

```python
import functools

import jax
import jax.numpy as jnp
from jax import lax
from jax.experimental import pallas as pl
from jax.experimental.pallas import tpu as pltpu
from jax.sharding import PartitionSpec as P

NX, NZ, NC = 2, 8, 2
NB = 8
EPS = 1e-05
BF16 = jnp.bfloat16
F32 = jnp.float32
OFFSETS = (4, 3, -3, 2, -2, 1, -1, 0)
FIRST = 2
VMEM_LIMIT = 56 * 1024 * 1024


def fsdp_index(x, z, core):
    return (x * NZ + z) * NC + core


def move(value, change):
    pairs = [
        (fsdp_index(x, z, c), fsdp_index(*change(x, z, c)))
        for x in range(NX)
        for z in range(NZ)
        for c in range(NC)
    ]
    return lax.ppermute(value, "fsdp", pairs)


def along_z(value, steps):
    return move(value, lambda x, z, c: (x, (z + steps) % NZ, c))


def swap_x(value):
    return move(value, lambda x, z, c: (1 - x, z, c))


def swap_core(value):
    return move(value, lambda x, z, c: (x, z, 1 - c))


def along_blk(value, steps, flip_x):
    size = NX * NZ * NC
    pairs = [
        (b * size + fsdp_index(x, z, c), ((b + steps) % NB) * size + fsdp_index(x ^ flip_x, z, c))
        for b in range(NB)
        for x in range(NX)
        for z in range(NZ)
        for c in range(NC)
    ]
    return lax.ppermute(value, ("blk", "fsdp"), pairs)


def params(**more):
    return pltpu.CompilerParams(vmem_limit_bytes=VMEM_LIMIT, **more)


def prepare_kernel(width, table, hidden, cot, scale, cot_t, send_a, send_b):
    rows = hidden.shape[0]
    total = jnp.zeros((rows, width), F32)
    for j in range(hidden.shape[1] // width):
        part = hidden[:, j * width:(j + 1) * width].astype(F32)
        total += part * part
    mean = jnp.sum(total, axis=1, keepdims=True) * (1.0 / hidden.shape[1])
    inverse = lax.rsqrt(mean + EPS)
    scale[...] = inverse
    cot_t[...] = (cot[...].astype(F32) * inverse).T.astype(BF16)
    for i in range(2 * len(OFFSETS)):
        start = pl.multiple_of((table[i] ^ 1) * width, width)
        part = hidden[:, pl.ds(start, width)]
        if i < 2 * FIRST:
            send_a[:, i * width:(i + 1) * width] = part
        else:
            j = i - 2 * FIRST
            send_b[:, j * width:(j + 1) * width] = part


def prepare(table, hidden, cot, width):
    tokens, features = hidden.shape
    values = cot.shape[1]
    step = 128
    first, rest = 2 * FIRST * width, 2 * (len(OFFSETS) - FIRST) * width
    row = lambda i, table: (i, 0)
    return pl.pallas_call(
        functools.partial(prepare_kernel, width),
        grid_spec=pltpu.PrefetchScalarGridSpec(
            num_scalar_prefetch=1,
            grid=(tokens // step,),
            in_specs=[pl.BlockSpec((step, features), row), pl.BlockSpec((step, values), row)],
            out_specs=[
                pl.BlockSpec((step, 1), row),
                pl.BlockSpec((values, step), lambda i, table: (0, i)),
                pl.BlockSpec((step, first), row),
                pl.BlockSpec((step, rest), row),
            ],
        ),
        out_shape=[
            jax.ShapeDtypeStruct((tokens, 1), F32),
            jax.ShapeDtypeStruct((values, tokens), BF16),
            jax.ShapeDtypeStruct((tokens, first), BF16),
            jax.ShapeDtypeStruct((tokens, rest), BF16),
        ],
        compiler_params=params(),
        cost_estimate=pl.CostEstimate(flops=3 * tokens * features, bytes_accessed=3 * tokens * features, transcendentals=0),
    )(table, hidden, cot)


def gradient_kernel(count, width, table, own_other, own_same, visiting, cot_t, cot_t_sibling, *outs):
    def part(own, at):
        total = jnp.dot(cot_t[...], own[...], preferred_element_type=F32)
        theirs = visiting[:, at * width:(at + 1) * width]
        return (total + jnp.dot(cot_t_sibling[...], theirs, preferred_element_type=F32)).astype(BF16)

    other, same = part(own_other, 0), part(own_same, 1)
    for i in range(count):
        @pl.when(pl.program_id(0) == i)
        def _():
            outs[2 * i][...] = other
            outs[2 * i + 1][...] = same


def gradient(table, hidden, visiting, cot_t, cot_t_sibling, base, count, width):
    tokens = hidden.shape[0]
    values = cot_t.shape[0]
    whole = pl.BlockSpec((values, tokens), lambda i, table: (0, 0))
    outs = pl.pallas_call(
        functools.partial(gradient_kernel, count, width),
        grid_spec=pltpu.PrefetchScalarGridSpec(
            num_scalar_prefetch=1,
            grid=(count,),
            in_specs=[
                pl.BlockSpec((tokens, width), lambda i, table: (0, table[2 * (base + i)])),
                pl.BlockSpec((tokens, width), lambda i, table: (0, table[2 * (base + i) + 1])),
                pl.BlockSpec((tokens, 2 * width), lambda i, table: (0, i)),
                whole,
                whole,
            ],
            out_specs=[pl.BlockSpec((values, width), lambda i, table: (0, 0))] * (2 * count),
        ),
        out_shape=[jax.ShapeDtypeStruct((values, width), BF16)] * (2 * count),
        compiler_params=params(),
        cost_estimate=pl.CostEstimate(
            flops=8 * count * tokens * values * width, bytes_accessed=8 * count * tokens * width + 4 * count * values * width, transcendentals=0
        ),
    )(table, hidden, hidden, visiting, cot_t, cot_t_sibling)
    return outs[0::2], outs[1::2]


def project_kernel(blocks, width, table, *refs):
    own = refs[:blocks]
    visit_a, visit_b = refs[blocks:blocks + 2]
    weights = refs[blocks + 2:-2]
    mine, theirs = refs[-2:]
    total = jnp.zeros(mine.shape, F32)
    total_theirs = jnp.zeros(theirs.shape, F32)
    at = 0
    for i in range(blocks):
        if i < 2 * FIRST:
            visitor = visit_a[:, i * width:(i + 1) * width]
        else:
            j = i - 2 * FIRST
            visitor = visit_b[:, j * width:(j + 1) * width]
        first = 0
        while first < width:
            weight = weights[at][...]
            last = first + weight.shape[0]
            total += jnp.dot(own[i][:, first:last], weight, preferred_element_type=F32)
            total_theirs += jnp.dot(visitor[:, first:last], weight, preferred_element_type=F32)
            first, at = last, at + 1
    mine[...] = total
    theirs[...] = total_theirs


def project(table, hidden, visit_a, visit_b, weights, width):
    tokens = hidden.shape[0]
    values = weights[0].shape[1]
    blocks = 2 * len(OFFSETS)
    step = 256 if tokens % 256 == 0 else tokens
    row = lambda t, table: (t, 0)
    specs = [pl.BlockSpec((step, width), lambda t, table, i=i: (t, table[i])) for i in range(blocks)]
    specs += [pl.BlockSpec((step, v.shape[1]), row) for v in (visit_a, visit_b)]
    specs += [pl.BlockSpec(w.shape, lambda t, table: (0, 0)) for w in weights]
    return pl.pallas_call(
        functools.partial(project_kernel, blocks, width),
        grid_spec=pltpu.PrefetchScalarGridSpec(
            num_scalar_prefetch=1,
            grid=(tokens // step,),
            in_specs=specs,
            out_specs=[pl.BlockSpec((step, values), row)] * 2,
        ),
        out_shape=[jax.ShapeDtypeStruct((tokens, values), F32)] * 2,
        compiler_params=params(),
        cost_estimate=pl.CostEstimate(
            flops=4 * tokens * blocks * width * values, bytes_accessed=4 * tokens * blocks * width + 2 * blocks * width * values, transcendentals=0
        ),
    )(table, *([hidden] * blocks), visit_a, visit_b, *weights)


def add(*terms):
    return sum(t.astype(F32) for t in terms).astype(BF16)


def per_device(hidden, gain, value_weight, cotangent, grad_weight_in, grad_gain_in):
    weight = value_weight[0].astype(F32)
    gains = gain[0].astype(F32)
    width = weight.shape[0]
    place = lax.axis_index("fsdp")
    core, z, x = place % NC, (place // NC) % NZ, place // (NC * NZ)
    table = jnp.stack(
        [fsdp_index(x ^ flip, (z + off + NZ) % NZ, core) for off in OFFSETS for flip in (1, 0)]
    ).astype(jnp.int32)

    scaled_weight = (weight * gains[:, None]).astype(BF16)
    layer = [along_blk(scaled_weight, 1, 0), along_blk(scaled_weight, 1, 1)]

    scale, cot_t, send_a, send_b = prepare(table, hidden, cotangent, width)
    visit_a = swap_core(send_a)
    cot_t_sibling = swap_core(cot_t)
    visit_b = swap_core(send_b)

    send_1, keep_1 = gradient(table, hidden, visit_a, cot_t, cot_t_sibling, 0, FIRST, width)
    send_2, keep_2 = gradient(table, hidden, visit_b, cot_t, cot_t_sibling, FIRST, len(OFFSETS) - FIRST, width)
    sends, keeps = [*send_1, *send_2], [*keep_1, *keep_2]
    arrived = [swap_x(s) for s in sends]
    mine = {off: (keeps[i], arrived[i]) for i, off in enumerate(OFFSETS)}

    half = sends[0].shape[0] // 2
    farthest = add(*mine[4])
    up = along_z(farthest[:half], 1)
    down = along_z(farthest[half:], -1)
    sum_up = jnp.concatenate([add(mine[3][0][:half], mine[3][1][:half], up), add(mine[3][0][half:], mine[3][1][half:])], axis=0)
    sum_down = jnp.concatenate([add(mine[-3][0][:half], mine[-3][1][:half]), add(mine[-3][0][half:], mine[-3][1][half:], down)], axis=0)
    for off in (2, 1, 0):
        up, down = along_z(sum_up, 1), along_z(sum_down, -1)
        if off:
            sum_up, sum_down = add(*mine[off], up), add(*mine[-off], down)
    total = along_blk(add(*mine[0], up, down), -1, 0)

    blocks = {(0, flip): [layer[flip]] for flip in (0, 1)}
    for flip in (0, 1):
        from_below, from_above = layer[flip], layer[flip]
        for step in (1, 2, 3):
            from_below, from_above = along_z(from_below, 1), along_z(from_above, -1)
            blocks[-step, flip], blocks[step, flip] = [from_below], [from_above]
        blocks[4, flip] = [along_z(from_below[:width // 2], 1), along_z(from_above[width // 2:], -1)]
    weights = [w for off in OFFSETS for flip in (1, 0) for w in blocks[off, flip]]
    product, product_sibling = project(table, hidden, visit_a, visit_b, weights, width)
    values = ((product + swap_core(product_sibling)) * scale).astype(BF16)

    summed = total.astype(F32).T
    grad_weight = grad_weight_in + (gains[:, None] * summed)[None]
    grad_gain = grad_gain_in + jnp.sum(weight * summed, axis=1)[None]
    return values, grad_weight, grad_gain


def solution(mesh):
    return jax.shard_map(
        per_device,
        mesh=mesh,
        in_specs=(
            P(("blk", "fsdp"), None),
            P("blk", "fsdp"),
            P("blk", "fsdp", None),
            P(("blk", "fsdp"), None),
            P("blk", "fsdp", None),
            P("blk", "fsdp"),
        ),
        out_specs=(P(("blk", "fsdp"), None), P("blk", "fsdp", None), P("blk", "fsdp")),
        check_vma=False,
    )
```

```python
import functools

import jax
import jax.numpy as jnp
from jax import lax
from jax.experimental import pallas as pl
from jax.experimental.pallas import tpu as pltpu
from jax.sharding import Mesh, PartitionSpec as P

NX, NZ, NC = 2, 8, 2
NB = 8
EPS = 1e-05
BF16 = jnp.bfloat16
F32 = jnp.float32
OFFSETS = (4, 3, -3, 2, -2, 1, -1, 0)
FIRST = 2
VMEM_LIMIT = 56 * 1024 * 1024


def fsdp_index(x, z, core):
    return (x * NZ + z) * NC + core


def move(value, change):
    pairs = [
        (fsdp_index(x, z, c), fsdp_index(*change(x, z, c)))
        for x in range(NX)
        for z in range(NZ)
        for c in range(NC)
    ]
    return lax.ppermute(value, ("x", "z", "core"), pairs)


def along_z(value, steps):
    return move(value, lambda x, z, c: (x, (z + steps) % NZ, c))


def swap_x(value):
    return move(value, lambda x, z, c: (1 - x, z, c))


def swap_core(value):
    return move(value, lambda x, z, c: (x, z, 1 - c))


def along_blk(value, steps, flip_x):
    size = NX * NZ * NC
    pairs = [
        (b * size + fsdp_index(x, z, c), ((b + steps) % NB) * size + fsdp_index(x ^ flip_x, z, c))
        for b in range(NB)
        for x in range(NX)
        for z in range(NZ)
        for c in range(NC)
    ]
    return lax.ppermute(value, ("blk", "x", "z", "core"), pairs)


def params(**more):
    return pltpu.CompilerParams(vmem_limit_bytes=VMEM_LIMIT, **more)


def prepare_kernel(width, table, hidden, cot, after, scale, cot_t, send_a, send_b):
    rows = hidden.shape[0]
    total = jnp.zeros((rows, width), F32)
    for j in range(hidden.shape[1] // width):
        part = hidden[:, j * width:(j + 1) * width].astype(F32)
        total += part * part
    mean = jnp.sum(total, axis=1, keepdims=True) * (1.0 / hidden.shape[1])
    inverse = lax.rsqrt(mean + EPS)
    scale[...] = inverse
    cot_t[...] = (cot[...].astype(F32) * inverse).T.astype(BF16)
    for i in range(2 * len(OFFSETS)):
        start = pl.multiple_of((table[i] ^ 1) * width, width)
        part = hidden[:, pl.ds(start, width)]
        if i < 2 * FIRST:
            send_a[:, i * width:(i + 1) * width] = part
        else:
            j = i - 2 * FIRST
            send_b[:, j * width:(j + 1) * width] = part


def prepare(table, hidden, cot, after, width):
    tokens, features = hidden.shape
    values = cot.shape[1]
    step = 128
    first, rest = 2 * FIRST * width, 2 * (len(OFFSETS) - FIRST) * width
    row = lambda i, table: (i, 0)
    return pl.pallas_call(
        functools.partial(prepare_kernel, width),
        grid_spec=pltpu.PrefetchScalarGridSpec(
            num_scalar_prefetch=1,
            grid=(tokens // step,),
            in_specs=[pl.BlockSpec((step, features), row), pl.BlockSpec((step, values), row), pl.BlockSpec(memory_space=pl.ANY)],
            out_specs=[
                pl.BlockSpec((step, 1), row),
                pl.BlockSpec((values, step), lambda i, table: (0, i)),
                pl.BlockSpec((step, first), row),
                pl.BlockSpec((step, rest), row),
            ],
        ),
        out_shape=[
            jax.ShapeDtypeStruct((tokens, 1), F32),
            jax.ShapeDtypeStruct((values, tokens), BF16),
            jax.ShapeDtypeStruct((tokens, first), BF16),
            jax.ShapeDtypeStruct((tokens, rest), BF16),
        ],
        compiler_params=params(),
        cost_estimate=pl.CostEstimate(flops=3 * tokens * features, bytes_accessed=3 * tokens * features, transcendentals=0),
    )(table, hidden, cot, after)


def gradient_kernel(count, width, table, own_other, own_same, visiting, cot_t, cot_t_sibling, *outs):
    def part(own, at):
        total = jnp.dot(cot_t[...], own[...], preferred_element_type=F32)
        theirs = visiting[:, at * width:(at + 1) * width]
        return (total + jnp.dot(cot_t_sibling[...], theirs, preferred_element_type=F32)).astype(BF16)

    other, same = part(own_other, 0), part(own_same, 1)
    for i in range(count):
        @pl.when(pl.program_id(0) == i)
        def _():
            outs[2 * i][...] = other
            outs[2 * i + 1][...] = same


def gradient(table, hidden, visiting, cot_t, cot_t_sibling, base, count, width):
    tokens = hidden.shape[0]
    values = cot_t.shape[0]
    whole = pl.BlockSpec((values, tokens), lambda i, table: (0, 0))
    outs = pl.pallas_call(
        functools.partial(gradient_kernel, count, width),
        grid_spec=pltpu.PrefetchScalarGridSpec(
            num_scalar_prefetch=1,
            grid=(count,),
            in_specs=[
                pl.BlockSpec((tokens, width), lambda i, table: (0, table[2 * (base + i)])),
                pl.BlockSpec((tokens, width), lambda i, table: (0, table[2 * (base + i) + 1])),
                pl.BlockSpec((tokens, 2 * width), lambda i, table: (0, i)),
                whole,
                whole,
            ],
            out_specs=[pl.BlockSpec((values, width), lambda i, table: (0, 0))] * (2 * count),
        ),
        out_shape=[jax.ShapeDtypeStruct((values, width), BF16)] * (2 * count),
        compiler_params=params(),
        cost_estimate=pl.CostEstimate(
            flops=8 * count * tokens * values * width, bytes_accessed=8 * count * tokens * width + 4 * count * values * width, transcendentals=0
        ),
    )(table, hidden, hidden, visiting, cot_t, cot_t_sibling)
    return outs[0::2], outs[1::2]


def project_kernel(width, table, own_other, own_same, visit_a, visit_b, weights, mine, theirs):
    step = pl.program_id(0)

    @pl.when(step == 0)
    def _():
        mine[...] = jnp.zeros_like(mine)
        theirs[...] = jnp.zeros_like(theirs)

    other, same = weights[0, 1], weights[0, 0]
    mine[...] += jnp.dot(own_other[...], other, preferred_element_type=F32) + jnp.dot(own_same[...], same, preferred_element_type=F32)

    def visitors(visit):
        theirs[...] += jnp.dot(visit[:, :width], other, preferred_element_type=F32) + jnp.dot(visit[:, width:], same, preferred_element_type=F32)

    pl.when(step < FIRST)(lambda: visitors(visit_a))
    pl.when(step >= FIRST)(lambda: visitors(visit_b))


def project(table, hidden, visit_a, visit_b, weights, width):
    tokens = hidden.shape[0]
    values = weights.shape[-1]
    count = len(OFFSETS)
    blocks = 2 * count
    out = pl.BlockSpec((tokens, values), lambda i, table: (0, 0))
    return pl.pallas_call(
        functools.partial(project_kernel, width),
        grid_spec=pltpu.PrefetchScalarGridSpec(
            num_scalar_prefetch=1,
            grid=(count,),
            in_specs=[
                pl.BlockSpec((tokens, width), lambda i, table: (0, table[2 * i])),
                pl.BlockSpec((tokens, width), lambda i, table: (0, table[2 * i + 1])),
                pl.BlockSpec((tokens, 2 * width), lambda i, table: (0, jnp.minimum(i, FIRST - 1))),
                pl.BlockSpec((tokens, 2 * width), lambda i, table: (0, jnp.maximum(i - FIRST, 0))),
                pl.BlockSpec((1, 2, width, values), lambda i, table: ((table[2 * i] // NC) % NZ, 0, 0, 0)),
            ],
            out_specs=[out, out],
        ),
        out_shape=[jax.ShapeDtypeStruct((tokens, values), F32)] * 2,
        compiler_params=params(),
        cost_estimate=pl.CostEstimate(
            flops=4 * tokens * blocks * width * values, bytes_accessed=4 * tokens * blocks * width + 2 * blocks * width * values, transcendentals=0
        ),
    )(table, hidden, hidden, visit_a, visit_b, weights)


def diagonal(width):
    return lax.broadcasted_iota(jnp.int32, (width, width), 0) == lax.broadcasted_iota(jnp.int32, (width, width), 1)


def as_column(row):
    return jnp.sum(jnp.where(diagonal(row.shape[1]), row, 0.0), axis=1, keepdims=True)


def as_row(column):
    return jnp.sum(jnp.where(diagonal(column.shape[0]), column, 0.0), axis=0, keepdims=True)


def scale_kernel(gain, weight, out):
    out[...] = (weight[0].astype(F32) * as_column(gain[...].astype(F32))).astype(BF16)


def scale_weight(gain, weight):
    return pl.pallas_call(scale_kernel, out_shape=jax.ShapeDtypeStruct(weight.shape[1:], BF16), compiler_params=params())(gain, weight)


def finish_kernel(total, gain, weight, grad_weight_in, grad_gain_in, grad_weight, grad_gain):
    summed = total[...].astype(F32).T
    grad_weight[0] = grad_weight_in[0] + as_column(gain[...].astype(F32)) * summed
    grad_gain[...] = grad_gain_in[...] + as_row(jnp.sum(weight[0].astype(F32) * summed, axis=1, keepdims=True))


def finish(total, gain, weight, grad_weight_in, grad_gain_in):
    return pl.pallas_call(
        finish_kernel,
        out_shape=[jax.ShapeDtypeStruct(a.shape, F32) for a in (grad_weight_in, grad_gain_in)],
        compiler_params=params(),
    )(total, gain, weight, grad_weight_in, grad_gain_in)


def add(*terms):
    return sum(t.astype(F32) for t in terms).astype(BF16)


def per_device(hidden, gain, value_weight, cotangent, grad_weight_in, grad_gain_in):
    width = value_weight.shape[1]
    x, z, core = (lax.axis_index(a) for a in ("x", "z", "core"))
    table = jnp.stack(
        [fsdp_index(x ^ flip, (z + off + NZ) % NZ, core) for off in OFFSETS for flip in (1, 0)]
    ).astype(jnp.int32)

    scaled_weight = scale_weight(gain, value_weight)
    layer = jnp.stack([along_blk(scaled_weight, 1, 0), along_blk(scaled_weight, 1, 1)])
    weights = lax.all_gather(layer, "z", axis=0)

    scale, cot_t, send_a, send_b = prepare(table, hidden, cotangent, scaled_weight, width)
    visit_a = swap_core(send_a)
    cot_t_sibling = swap_core(cot_t)
    visit_b = swap_core(send_b)

    send_1, keep_1 = gradient(table, hidden, visit_a, cot_t, cot_t_sibling, 0, FIRST, width)
    send_2, keep_2 = gradient(table, hidden, visit_b, cot_t, cot_t_sibling, FIRST, len(OFFSETS) - FIRST, width)
    sends, keeps = [*send_1, *send_2], [*keep_1, *keep_2]
    arrived = [swap_x(s) for s in sends]
    mine = {off: (keeps[i], arrived[i]) for i, off in enumerate(OFFSETS)}

    half = sends[0].shape[0] // 2
    farthest = add(*mine[4])
    up = along_z(farthest[:half], 1)
    down = along_z(farthest[half:], -1)
    sum_up = jnp.concatenate([add(mine[3][0][:half], mine[3][1][:half], up), add(mine[3][0][half:], mine[3][1][half:])], axis=0)
    sum_down = jnp.concatenate([add(mine[-3][0][:half], mine[-3][1][:half]), add(mine[-3][0][half:], mine[-3][1][half:], down)], axis=0)
    for off in (2, 1, 0):
        up, down = along_z(sum_up, 1), along_z(sum_down, -1)
        if off:
            sum_up, sum_down = add(*mine[off], up), add(*mine[-off], down)
    total = along_blk(add(*mine[0], up, down), -1, 0)

    product, product_sibling = project(table, hidden, visit_a, visit_b, weights, width)
    values = ((product + swap_core(product_sibling)) * scale).astype(BF16)

    return values, *finish(total, gain, value_weight, grad_weight_in, grad_gain_in)


def solution(mesh):
    fsdp = ("x", "z", "core")
    return jax.shard_map(
        per_device,
        mesh=Mesh(mesh.devices.reshape(NB, NX, NZ, NC), ("blk", *fsdp)),
        in_specs=(
            P(("blk", *fsdp), None),
            P("blk", fsdp),
            P("blk", fsdp, None),
            P(("blk", *fsdp), None),
            P("blk", fsdp, None),
            P("blk", fsdp),
        ),
        out_specs=(P(("blk", *fsdp), None), P("blk", fsdp, None), P("blk", fsdp)),
        check_vma=False,
    )
```

```python
import functools

import jax
import jax.numpy as jnp
from jax import lax
from jax.experimental import pallas as pl
from jax.experimental.pallas import tpu as pltpu
from jax.sharding import Mesh, PartitionSpec as P

NX, NZ, NC = 2, 8, 2
NB = 8
EPS = 1e-05
BF16 = jnp.bfloat16
F32 = jnp.float32
OFFSETS = (4, 3, -3, 2, -2, 1, -1, 0)
FIRST = 2
VMEM_LIMIT = 16 * 1024 * 1024
LOAD_LIMIT = 47 * 1024 * 1024


def fsdp_index(x, z, core):
    return (x * NZ + z) * NC + core


def move(value, change):
    pairs = [
        (fsdp_index(x, z, c), fsdp_index(*change(x, z, c)))
        for x in range(NX)
        for z in range(NZ)
        for c in range(NC)
    ]
    return lax.ppermute(value, ("x", "z", "core"), pairs)


def along_z(value, steps):
    return move(value, lambda x, z, c: (x, (z + steps) % NZ, c))


def swap_x(value):
    return move(value, lambda x, z, c: (1 - x, z, c))


def swap_core(value):
    return move(value, lambda x, z, c: (x, z, 1 - c))


def along_blk(value, steps, flip_x):
    size = NX * NZ * NC
    pairs = [
        (b * size + fsdp_index(x, z, c), ((b + steps) % NB) * size + fsdp_index(x ^ flip_x, z, c))
        for b in range(NB)
        for x in range(NX)
        for z in range(NZ)
        for c in range(NC)
    ]
    return lax.ppermute(value, ("blk", "x", "z", "core"), pairs)


def params(limit=VMEM_LIMIT):
    return pltpu.CompilerParams(vmem_limit_bytes=limit)


def cost(flops, size):
    return pl.CostEstimate(flops=flops, bytes_accessed=size, transcendentals=0)


IN_VMEM = pl.BlockSpec(memory_space=pltpu.VMEM)
IN_SMEM = pl.BlockSpec(memory_space=pltpu.SMEM)
ANYWHERE = pl.BlockSpec(memory_space=pl.ANY)
IN_HBM = pl.BlockSpec(memory_space=pltpu.HBM)


def block(ref, index, width):
    return ref[:, pl.ds(pl.multiple_of(index * width, width), width)]


def prepare_kernel(width, steps, table, hidden, cot, after, scale, cot_t, send_a, send_b, held, arrivals):
    step = hidden.shape[0] // steps
    lanes = 128
    copies = []
    for at in range(steps):
        rows = pl.ds(at * step, step)
        copy = pltpu.make_async_copy(hidden.at[rows, :], held.at[rows, :], arrivals.at[at])
        copy.start()
        copies.append(copy)
    first = send_a.shape[1] // width
    for at in range(steps):
        copies[at].wait()
        rows = slice(at * step, (at + 1) * step)
        total = jnp.zeros((step, lanes), F32)
        for j in range(hidden.shape[1] // lanes):
            part = held[rows, j * lanes:(j + 1) * lanes].astype(F32)
            total += part * part
        inverse = lax.rsqrt(jnp.sum(total, axis=1, keepdims=True) * (1.0 / hidden.shape[1]) + EPS)
        scale[rows, :] = inverse
        cot_t[:, rows] = (cot[rows, :].astype(F32) * inverse).T.astype(BF16)
        for i in range(first + send_b.shape[1] // width):
            out, j = (send_a, i) if i < first else (send_b, i - first)
            start = pl.multiple_of((table[i] ^ 1) * width, width)
            out[rows, j * width:(j + 1) * width] = held[rows, pl.ds(start, width)]


def prepare(table, hidden, cot, after, width):
    tokens, features = hidden.shape
    values = cot.shape[1]
    steps = 4
    return pl.pallas_call(
        functools.partial(prepare_kernel, width, steps),
        in_specs=[IN_SMEM, IN_HBM, IN_VMEM, ANYWHERE],
        out_specs=[IN_VMEM] * 4,
        out_shape=[
            jax.ShapeDtypeStruct((tokens, 1), F32),
            jax.ShapeDtypeStruct((values, tokens), BF16),
            jax.ShapeDtypeStruct((tokens, 2 * FIRST * width), BF16),
            jax.ShapeDtypeStruct((tokens, 2 * (len(OFFSETS) - FIRST) * width), BF16),
        ],
        scratch_shapes=[pltpu.VMEM((tokens, features), BF16), pltpu.SemaphoreType.DMA((steps,))],
        compiler_params=params(LOAD_LIMIT),
        cost_estimate=cost(0, tokens),
    )(table, hidden, cot, after)


def gradient_kernel(base, width, table, hidden, visiting, cot_t, cot_t_sibling, *outs):
    for i, out in enumerate(outs):
        total = jnp.dot(cot_t[...], block(hidden, table[2 * base + i], width), preferred_element_type=F32)
        theirs = visiting[:, i * width:(i + 1) * width]
        out[...] = (total + jnp.dot(cot_t_sibling[...], theirs, preferred_element_type=F32)).astype(BF16)


def gradient(table, hidden, visiting, cot_t, cot_t_sibling, base, count, width):
    tokens = hidden.shape[0]
    values = cot_t.shape[0]
    outs = pl.pallas_call(
        functools.partial(gradient_kernel, base, width),
        in_specs=[IN_SMEM] + [IN_VMEM] * 4,
        out_specs=[IN_VMEM] * (2 * count),
        out_shape=[jax.ShapeDtypeStruct((values, width), BF16)] * (2 * count),
        compiler_params=params(),
        cost_estimate=cost(8 * count * tokens * values * width, 8 * count * tokens * width + 4 * count * values * width),
    )(table, hidden, visiting, cot_t, cot_t_sibling)
    return outs[0::2], outs[1::2]


def project_kernel(width, table, hidden, visit_a, visit_b, weights, mine, theirs):
    for i in range(0, len(OFFSETS), 2):
        near, far = ((table[2 * j] // NC) % NZ for j in (i, i + 1))
        weight = jnp.concatenate([weights[z].reshape(2 * width, mine.shape[1]) for z in (near, far)], axis=0)
        own = jnp.concatenate([block(hidden, table[2 * i + j], width) for j in range(4)], axis=1)
        visit, at = (visit_a, 2 * i * width) if i < FIRST else (visit_b, 2 * (i - FIRST) * width)
        product = jnp.dot(own, weight, preferred_element_type=F32)
        product_theirs = jnp.dot(visit[:, at:at + 4 * width], weight, preferred_element_type=F32)
        if i:
            mine[...] += product
            theirs[...] += product_theirs
        else:
            mine[...] = product
            theirs[...] = product_theirs


def project(table, hidden, visit_a, visit_b, weights, width):
    tokens = hidden.shape[0]
    values = weights.shape[-1]
    size = weights.size
    return pl.pallas_call(
        functools.partial(project_kernel, width),
        in_specs=[IN_SMEM] + [IN_VMEM] * 4,
        out_specs=[IN_VMEM, IN_VMEM],
        out_shape=[jax.ShapeDtypeStruct((tokens, values), F32)] * 2,
        compiler_params=params(),
        cost_estimate=cost(4 * tokens * size, 2 * size),
    )(table, hidden, visit_a, visit_b, weights)


def pair_kernel(one, other, after, out):
    out[0] = one[...]
    out[1] = other[...]


def pair(one, other, after):
    return pl.pallas_call(
        pair_kernel,
        in_specs=[IN_VMEM, IN_VMEM, ANYWHERE],
        out_specs=IN_VMEM,
        out_shape=jax.ShapeDtypeStruct((2, *one.shape), one.dtype),
        compiler_params=params(),
        cost_estimate=cost(0, 8 * one.size),
    )(one, other, after)


def halves_kernel(one, other, after, upper, lower):
    half = upper.shape[0]
    upper[...] = (one[:half].astype(F32) + other[:half].astype(F32)).astype(BF16)
    lower[...] = (one[half:].astype(F32) + other[half:].astype(F32)).astype(BF16)


def halves(one, other, after):
    half = jax.ShapeDtypeStruct((one.shape[0] // 2, one.shape[1]), BF16)
    return pl.pallas_call(
        halves_kernel,
        in_specs=[IN_VMEM, IN_VMEM, ANYWHERE],
        out_specs=[IN_VMEM, IN_VMEM],
        out_shape=[half, half],
        compiler_params=params(),
        cost_estimate=cost(one.size, 6 * one.size),
    )(one, other, after)


def diagonal(width):
    return lax.broadcasted_iota(jnp.int32, (width, width), 0) == lax.broadcasted_iota(jnp.int32, (width, width), 1)


def as_column(row):
    return jnp.sum(jnp.where(diagonal(row.shape[1]), row, 0.0), axis=1, keepdims=True)


def as_row(column):
    return jnp.sum(jnp.where(diagonal(column.shape[0]), column, 0.0), axis=0, keepdims=True)


def scale_kernel(gain, weight, out):
    out[...] = (weight[0].astype(F32) * as_column(gain[...].astype(F32))).astype(BF16)


def scale_weight(gain, weight):
    return pl.pallas_call(scale_kernel, out_shape=jax.ShapeDtypeStruct(weight.shape[1:], BF16), compiler_params=params())(gain, weight)


def finish_kernel(total, gain, weight, grad_weight_in, grad_gain_in, grad_weight, grad_gain):
    summed = total[...].astype(F32).T
    grad_weight[0] = grad_weight_in[0] + as_column(gain[...].astype(F32)) * summed
    grad_gain[...] = grad_gain_in[...] + as_row(jnp.sum(weight[0].astype(F32) * summed, axis=1, keepdims=True))


def finish(total, gain, weight, grad_weight_in, grad_gain_in):
    return pl.pallas_call(
        finish_kernel,
        out_shape=[jax.ShapeDtypeStruct(a.shape, F32) for a in (grad_weight_in, grad_gain_in)],
        compiler_params=params(),
    )(total, gain, weight, grad_weight_in, grad_gain_in)


def add(*terms):
    return sum(t.astype(F32) for t in terms).astype(BF16)


def per_device(hidden, gain, value_weight, cotangent, grad_weight_in, grad_gain_in):
    width = value_weight.shape[1]
    x, z, core = (lax.axis_index(a) for a in ("x", "z", "core"))
    table = jnp.stack(
        [fsdp_index(x ^ flip, (z + off + NZ) % NZ, core) for off in OFFSETS for flip in (0, 1)]
    ).astype(jnp.int32)

    scaled_weight = scale_weight(gain, value_weight)
    layer = [along_blk(scaled_weight, 1, flip) for flip in (0, 1)]

    rest = len(OFFSETS) - FIRST
    scale, cot_t, send_a, send_b = prepare(table, hidden, cotangent, scaled_weight, width)
    cot_t_sibling, visit_a, visit_b = (swap_core(a) for a in (cot_t, send_a, send_b))
    weights = lax.all_gather(pair(*layer, cot_t), "z", axis=0)

    keep_1, send_1 = gradient(table, hidden, visit_a, cot_t, cot_t_sibling, 0, FIRST, width)
    keep_2, send_2 = gradient(table, hidden, visit_b, cot_t, cot_t_sibling, FIRST, rest, width)
    sends, keeps = [*send_1, *send_2], [*keep_1, *keep_2]
    arrived = [swap_x(s) for s in sends]
    mine = {off: (keeps[i], arrived[i]) for i, off in enumerate(OFFSETS)}

    half = sends[0].shape[0] // 2
    upper, lower = halves(*mine[4], send_2[-1])
    up, down = along_z(upper, 1), along_z(lower, -1)
    sum_up = jnp.concatenate([add(mine[3][0][:half], mine[3][1][:half], up), add(mine[3][0][half:], mine[3][1][half:])], axis=0)
    sum_down = jnp.concatenate([add(mine[-3][0][:half], mine[-3][1][:half]), add(mine[-3][0][half:], mine[-3][1][half:], down)], axis=0)
    for off in (2, 1, 0):
        up, down = along_z(sum_up, 1), along_z(sum_down, -1)
        if off:
            sum_up, sum_down = add(*mine[off], up), add(*mine[-off], down)
    total = along_blk(add(*mine[0], up, down), -1, 0)

    product, product_sibling = project(table, hidden, visit_a, visit_b, weights, width)
    values = ((product + swap_core(product_sibling)) * scale).astype(BF16)

    return values, *finish(total, gain, value_weight, grad_weight_in, grad_gain_in)


def solution(mesh):
    fsdp = ("x", "z", "core")
    return jax.shard_map(
        per_device,
        mesh=Mesh(mesh.devices.reshape(NB, NX, NZ, NC), ("blk", *fsdp)),
        in_specs=(
            P(("blk", *fsdp), None),
            P("blk", fsdp),
            P("blk", fsdp, None),
            P(("blk", *fsdp), None),
            P("blk", fsdp, None),
            P("blk", fsdp),
        ),
        out_specs=(P(("blk", *fsdp), None), P("blk", fsdp, None), P("blk", fsdp)),
        check_vma=False,
    )
```

```python
import functools

import jax
import jax.numpy as jnp
from jax import lax
from jax.experimental import pallas as pl
from jax.experimental.pallas import tpu as pltpu
from jax.sharding import Mesh, PartitionSpec as P

NX, NZ, NC = 2, 8, 2
NB = 8
EPS = 1e-05
BF16 = jnp.bfloat16
F32 = jnp.float32
OFFSETS = (4, 3, -3, 2, -2, 1, -1, 0)
FIRST = 2
VMEM_LIMIT = 16 * 1024 * 1024
LOAD_LIMIT = 36 * 1024 * 1024


def fsdp_index(x, z, core):
    return (x * NZ + z) * NC + core


def move(value, change):
    pairs = [
        (fsdp_index(x, z, c), fsdp_index(*change(x, z, c)))
        for x in range(NX)
        for z in range(NZ)
        for c in range(NC)
    ]
    return lax.ppermute(value, ("x", "z", "core"), pairs)


def along_z(value, steps):
    return move(value, lambda x, z, c: (x, (z + steps) % NZ, c))


def swap_x(value):
    return move(value, lambda x, z, c: (1 - x, z, c))


def swap_core(value):
    return move(value, lambda x, z, c: (x, z, 1 - c))


def along_blk(value, steps, flip_x):
    size = NX * NZ * NC
    pairs = [
        (b * size + fsdp_index(x, z, c), ((b + steps) % NB) * size + fsdp_index(x ^ flip_x, z, c))
        for b in range(NB)
        for x in range(NX)
        for z in range(NZ)
        for c in range(NC)
    ]
    return lax.ppermute(value, ("blk", "x", "z", "core"), pairs)


def params(limit=VMEM_LIMIT):
    return pltpu.CompilerParams(vmem_limit_bytes=limit)


def cost(flops, size):
    return pl.CostEstimate(flops=flops, bytes_accessed=size, transcendentals=0)


IN_VMEM = pl.BlockSpec(memory_space=pltpu.VMEM)
IN_SMEM = pl.BlockSpec(memory_space=pltpu.SMEM)
ANYWHERE = pl.BlockSpec(memory_space=pl.ANY)
IN_HBM = pl.BlockSpec(memory_space=pltpu.HBM)


def block(ref, index, width):
    return ref[:, pl.ds(pl.multiple_of(index * width, width), width)]


def prepare_kernel(width, steps, table, hidden, cot, after, held, scale, cot_t, send_a, send_b, arrivals):
    step = hidden.shape[0] // steps
    lanes = 128
    copies = []
    for at in range(steps):
        rows = pl.ds(at * step, step)
        copy = pltpu.make_async_copy(hidden.at[rows, :], held.at[rows, :], arrivals.at[at])
        copy.start()
        copies.append(copy)
    first = send_a.shape[1] // width
    for at in range(steps):
        copies[at].wait()
        rows = slice(at * step, (at + 1) * step)
        total = jnp.zeros((step, lanes), F32)
        for j in range(hidden.shape[1] // lanes):
            part = held[rows, j * lanes:(j + 1) * lanes].astype(F32)
            total += part * part
        inverse = lax.rsqrt(jnp.sum(total, axis=1, keepdims=True) * (1.0 / hidden.shape[1]) + EPS)
        scale[rows, :] = inverse
        cot_t[:, rows] = (cot[rows, :].astype(F32) * inverse).T.astype(BF16)
        for i in range(first + send_b.shape[1] // width):
            out, j = (send_a, i) if i < first else (send_b, i - first)
            start = pl.multiple_of((table[i] ^ 1) * width, width)
            out[rows, j * width:(j + 1) * width] = held[rows, pl.ds(start, width)]


def prepare(table, hidden, cot, after, width):
    tokens, features = hidden.shape
    values = cot.shape[1]
    steps = 4
    return pl.pallas_call(
        functools.partial(prepare_kernel, width, steps),
        in_specs=[IN_SMEM, IN_HBM, IN_VMEM, ANYWHERE],
        out_specs=[IN_VMEM] * 5,
        out_shape=[
            jax.ShapeDtypeStruct((tokens, features), BF16),
            jax.ShapeDtypeStruct((tokens, 1), F32),
            jax.ShapeDtypeStruct((values, tokens), BF16),
            jax.ShapeDtypeStruct((tokens, 2 * FIRST * width), BF16),
            jax.ShapeDtypeStruct((tokens, 2 * (len(OFFSETS) - FIRST) * width), BF16),
        ],
        scratch_shapes=[pltpu.SemaphoreType.DMA((steps,))],
        compiler_params=params(LOAD_LIMIT),
        cost_estimate=cost(0, tokens),
    )(table, hidden, cot, after)


def gradient_kernel(base, groups, width, table, hidden, visiting, cot_t, cot_t_sibling, *outs):
    at = base
    sends = iter(outs[:len(groups)])
    keeps = iter(outs[len(groups):])
    for size in groups:
        send = next(sends)
        for j in range(size):
            for flip in (1, 0):
                total = jnp.dot(cot_t[...], block(hidden, table[2 * at + flip], width), preferred_element_type=F32)
                i = 2 * (at - base) + flip
                theirs = visiting[:, i * width:(i + 1) * width]
                total = (total + jnp.dot(cot_t_sibling[...], theirs, preferred_element_type=F32)).astype(BF16)
                if flip:
                    send[j] = total
                else:
                    next(keeps)[...] = total
            at += 1


def gradient(table, hidden, visiting, cot_t, cot_t_sibling, base, groups, width):
    tokens = hidden.shape[0]
    values = cot_t.shape[0]
    count = sum(groups)
    outs = pl.pallas_call(
        functools.partial(gradient_kernel, base, groups, width),
        in_specs=[IN_SMEM] + [IN_VMEM] * 4,
        out_specs=[IN_VMEM] * (len(groups) + count),
        out_shape=[jax.ShapeDtypeStruct((size, values, width), BF16) for size in groups]
        + [jax.ShapeDtypeStruct((values, width), BF16)] * count,
        compiler_params=params(),
        cost_estimate=cost(8 * count * tokens * values * width, 8 * count * tokens * width + 4 * count * values * width),
    )(table, hidden, visiting, cot_t, cot_t_sibling)
    return outs[:len(groups)], outs[len(groups):]


def project_kernel(offsets, sizes, more, width, table, hidden, visit_a, visit_b, *refs):
    mine, theirs = refs[-2:]
    start = refs[-4:-2] if more else None
    refs = iter(refs)
    weights = [[next(refs) for _ in range(size)] for size in sizes]
    product = product_theirs = None
    for at in range(0, len(offsets), 2):
        chosen = [OFFSETS.index(off) for off in offsets[at:at + 2]]
        weight = [ref[...].reshape(-1, mine.shape[1]) for group in weights[at:at + 2] for ref in group]
        weight = jnp.concatenate(weight, axis=0)
        own = jnp.concatenate([block(hidden, table[2 * i + flip], width) for i in chosen for flip in (0, 1)], axis=1)
        visitors = []
        for i in chosen:
            visit, j = (visit_a, i) if i < FIRST else (visit_b, i - FIRST)
            visitors.append(visit[:, 2 * j * width:2 * (j + 1) * width])
        visitors = jnp.concatenate(visitors, axis=1)
        product = jnp.dot(own, weight, preferred_element_type=F32)
        product_theirs = jnp.dot(visitors, weight, preferred_element_type=F32)
        if at:
            mine[...] += product
            theirs[...] += product_theirs
        elif more:
            mine[...] = start[0][...] + product
            theirs[...] = start[1][...] + product_theirs
        else:
            mine[...] = product
            theirs[...] = product_theirs


def project(table, hidden, visit_a, visit_b, weights, start, width):
    tokens = hidden.shape[0]
    values = hidden.shape[0] if start is None else start[0].shape[1]
    arrays = [w for group in weights.values() for w in group]
    values = arrays[0].shape[-1]
    size = sum(w.size for w in arrays)
    more = [] if start is None else list(start)
    return pl.pallas_call(
        functools.partial(project_kernel, tuple(weights), [len(g) for g in weights.values()], bool(more), width),
        in_specs=[IN_SMEM] + [IN_VMEM] * (3 + len(arrays) + len(more)),
        out_specs=[IN_VMEM, IN_VMEM],
        out_shape=[jax.ShapeDtypeStruct((tokens, values), F32)] * 2,
        compiler_params=params(),
        cost_estimate=cost(4 * tokens * size, 2 * size),
    )(table, hidden, visit_a, visit_b, *arrays, *more)


def small(kernel, inputs, after, shapes, dtype=BF16):
    def body(*refs):
        kernel(*refs[:len(inputs)], *refs[len(inputs) + len(after):])

    return pl.pallas_call(
        body,
        in_specs=[IN_VMEM] * len(inputs) + [ANYWHERE] * len(after),
        out_specs=[IN_VMEM] * len(shapes),
        out_shape=[jax.ShapeDtypeStruct(shape, dtype) for shape in shapes],
        compiler_params=params(),
        cost_estimate=cost(0, sum(a.size * a.dtype.itemsize for a in inputs)),
    )(*inputs, *after)


def pair(one, other, after):
    def kernel(one, other, out):
        out[0] = one[...]
        out[1] = other[...]

    return small(kernel, [one, other], after, [(2, *one.shape)])[0]


def split(pair_up, pair_down):
    def kernel(up, down, out_up, out_down):
        out_up[...] = up[0]
        out_down[...] = down[1]

    return small(kernel, [pair_up, pair_down], [], [pair_up.shape[1:]] * 2)


def total_of(terms, rows=slice(None)):
    return sum(t[rows].astype(F32) for t in terms).astype(BF16)


def begin(terms, places, after):
    values, width = terms[0].shape
    half = values // 2

    def kernel(keep, arrived, upper, lower):
        parts = (keep, arrived.at[places[0]])
        upper[...] = total_of(parts, slice(0, half))
        lower[...] = total_of(parts, slice(half, values))

    return small(kernel, terms, after, [(half, width)] * 2)


def carry(ups, downs, places, after):
    values, width = ups[0].shape

    def kernel(keep_up, arrived_up, up, keep_down, arrived_down, down, out_up, out_down):
        up_parts = (keep_up, arrived_up.at[places[0]])
        down_parts = (keep_down, arrived_down.at[places[1]])
        if up.shape[0] == values:
            out_up[...] = total_of((*up_parts, up))
            out_down[...] = total_of((*down_parts, down))
        else:
            half = values // 2
            upper, lower = slice(0, half), slice(half, values)
            out_up[upper, :] = (sum(t[upper].astype(F32) for t in up_parts) + up[...].astype(F32)).astype(BF16)
            out_up[lower, :] = total_of(up_parts, lower)
            out_down[upper, :] = total_of(down_parts, upper)
            out_down[lower, :] = (sum(t[lower].astype(F32) for t in down_parts) + down[...].astype(F32)).astype(BF16)

    return small(kernel, [*ups, *downs], after, [(values, width)] * 2)


def end(terms, place):
    def kernel(keep, arrived, up, down, out):
        out[...] = total_of((keep, arrived.at[place], up, down))

    return small(kernel, terms, [], [terms[0].shape])[0]


def scaled_values(product, arrived, scale):
    def kernel(product, arrived, scale, out):
        out[...] = ((product[...] + arrived[...]) * scale[...]).astype(BF16)

    return small(kernel, [product, arrived, scale], [], [product.shape])[0]


def diagonal(width):
    return lax.broadcasted_iota(jnp.int32, (width, width), 0) == lax.broadcasted_iota(jnp.int32, (width, width), 1)


def as_column(row):
    return jnp.sum(jnp.where(diagonal(row.shape[1]), row, 0.0), axis=1, keepdims=True)


def as_row(column):
    return jnp.sum(jnp.where(diagonal(column.shape[0]), column, 0.0), axis=0, keepdims=True)


def scale_kernel(gain, weight, out):
    out[...] = (weight[0].astype(F32) * as_column(gain[...].astype(F32))).astype(BF16)


def scale_weight(gain, weight):
    return pl.pallas_call(scale_kernel, out_shape=jax.ShapeDtypeStruct(weight.shape[1:], BF16), compiler_params=params())(gain, weight)


def finish_kernel(total, gain, weight, grad_weight_in, grad_gain_in, grad_weight, grad_gain):
    summed = total[...].astype(F32).T
    grad_weight[0] = grad_weight_in[0] + as_column(gain[...].astype(F32)) * summed
    grad_gain[...] = grad_gain_in[...] + as_row(jnp.sum(weight[0].astype(F32) * summed, axis=1, keepdims=True))


def finish(total, gain, weight, grad_weight_in, grad_gain_in):
    return pl.pallas_call(
        finish_kernel,
        out_shape=[jax.ShapeDtypeStruct(a.shape, F32) for a in (grad_weight_in, grad_gain_in)],
        compiler_params=params(),
    )(total, gain, weight, grad_weight_in, grad_gain_in)


def per_device(hidden, gain, value_weight, cotangent, grad_weight_in, grad_gain_in):
    width = value_weight.shape[1]
    x, z, core = (lax.axis_index(a) for a in ("x", "z", "core"))
    table = jnp.stack(
        [fsdp_index(x ^ flip, (z + off + NZ) % NZ, core) for off in OFFSETS for flip in (0, 1)]
    ).astype(jnp.int32)

    scaled_weight = scale_weight(gain, value_weight)
    layer = [along_blk(scaled_weight, 1, flip) for flip in (0, 1)]

    rest = len(OFFSETS) - FIRST
    held, scale, cot_t, send_a, send_b = prepare(table, hidden, cotangent, scaled_weight, width)
    cot_t_sibling, visit_a, visit_b = (swap_core(a) for a in (cot_t, send_a, send_b))

    pairs = (len(OFFSETS) - FIRST) // 2
    sends_1, keeps_1 = gradient(table, held, visit_a, cot_t, cot_t_sibling, 0, (1,) * FIRST, width)
    sends_2, keeps_2 = gradient(table, held, visit_b, cot_t, cot_t_sibling, FIRST, (2,) * pairs, width)
    arrived = [swap_x(send) for send in (*sends_1, *sends_2)]
    keeps = [*keeps_1, *keeps_2]
    places = [(i, 0) for i in range(FIRST)] + [(FIRST + i, j) for i in range(pairs) for j in (0, 1)]
    mine = {off: (keeps[i], arrived[places[i][0]]) for i, off in enumerate(OFFSETS)}
    place = {off: places[i][1] for i, off in enumerate(OFFSETS)}

    layer = pair(*layer, [cot_t])
    up, down = begin(mine[4], (place[4],), [sends_2[-1]])
    weights = {0: [layer]}
    layer_up = layer_down = layer
    for step in (1, 2, 3):
        layer_up, layer_down = along_z(layer_up, 1), along_z(layer_down, -1)
        weights[-step], weights[step] = [layer_up], [layer_down]
        off = 4 - step
        up, down = along_z(up, 1), along_z(down, -1)
        up, down = carry((*mine[off], up), (*mine[-off], down), (place[off], place[-off]), [layer_up, layer_down])
    far_up, far_down = split(layer_up, layer_down)
    weights[4] = [along_z(far_up, 1), along_z(far_down, -1)]
    up, down = along_z(up, 1), along_z(down, -1)
    total = along_blk(end((*mine[0], up, down), place[0]), -1, 0)

    near = {off: weights[off] for off in (0, -1, 1, -2, 2)}
    far = {off: weights[off] for off in (-3, 3, 4)}
    products = project(table, held, visit_a, visit_b, near, None, width)
    product, product_sibling = project(table, held, visit_a, visit_b, far, products, width)
    values = scaled_values(product, swap_core(product_sibling), scale)

    return values, *finish(total, gain, value_weight, grad_weight_in, grad_gain_in)


def solution(mesh):
    fsdp = ("x", "z", "core")
    return jax.shard_map(
        per_device,
        mesh=Mesh(mesh.devices.reshape(NB, NX, NZ, NC), ("blk", *fsdp)),
        in_specs=(
            P(("blk", *fsdp), None),
            P("blk", fsdp),
            P("blk", fsdp, None),
            P(("blk", *fsdp), None),
            P("blk", fsdp, None),
            P("blk", fsdp),
        ),
        out_specs=(P(("blk", *fsdp), None), P("blk", fsdp, None), P("blk", fsdp)),
        check_vma=False,
    )
```

```python
import functools

import jax
import jax.numpy as jnp
from jax import lax
from jax.experimental import pallas as pl
from jax.experimental.pallas import tpu as pltpu
from jax.sharding import Mesh, PartitionSpec as P

NX, NZ, NC = 2, 8, 2
NB = 8
EPS = 1e-05
BF16 = jnp.bfloat16
F32 = jnp.float32
OFFSETS = (4, 3, -3, 2, -2, 1, -1, 0)
GROUPS = ((1, 2), (2, 2, 1))
FIRST = sum(GROUPS[0])
SWAPS = (3, 2, 3)
VMEM_LIMIT = 16 * 1024 * 1024
LOAD_LIMIT = 36 * 1024 * 1024


def fsdp_index(x, z, core):
    return (x * NZ + z) * NC + core


def move(value, change):
    pairs = [
        (fsdp_index(x, z, c), fsdp_index(*change(x, z, c)))
        for x in range(NX)
        for z in range(NZ)
        for c in range(NC)
    ]
    return lax.ppermute(value, ("x", "z", "core"), pairs)


def along_z(value, steps):
    return move(value, lambda x, z, c: (x, (z + steps) % NZ, c))


def swap_x(value):
    return move(value, lambda x, z, c: (1 - x, z, c))


def swap_core(value):
    return move(value, lambda x, z, c: (x, z, 1 - c))


def along_blk(value, steps, flip_x):
    size = NX * NZ * NC
    pairs = [
        (b * size + fsdp_index(x, z, c), ((b + steps) % NB) * size + fsdp_index(x ^ flip_x, z, c))
        for b in range(NB)
        for x in range(NX)
        for z in range(NZ)
        for c in range(NC)
    ]
    return lax.ppermute(value, ("blk", "x", "z", "core"), pairs)


def params(limit=VMEM_LIMIT):
    return pltpu.CompilerParams(vmem_limit_bytes=limit)


def cost(flops, size):
    return pl.CostEstimate(flops=flops, bytes_accessed=size, transcendentals=0)


IN_VMEM = pl.BlockSpec(memory_space=pltpu.VMEM)
IN_SMEM = pl.BlockSpec(memory_space=pltpu.SMEM)
ANYWHERE = pl.BlockSpec(memory_space=pl.ANY)
IN_HBM = pl.BlockSpec(memory_space=pltpu.HBM)


def block(ref, index, width):
    return ref[:, pl.ds(pl.multiple_of(index * width, width), width)]


def swapped(visits, index, width):
    for visit, size in zip(visits, SWAPS):
        if index < size:
            return visit[:, 2 * index * width:2 * (index + 1) * width]
        index -= size


def prepare_kernel(width, steps, table, hidden, cot, after, held, scale, cot_t, *rest):
    sends, arrivals = rest[:-1], rest[-1]
    step = hidden.shape[0] // steps
    lanes = 128
    copies = []
    for at in range(steps):
        rows = pl.ds(at * step, step)
        copy = pltpu.make_async_copy(hidden.at[rows, :], held.at[rows, :], arrivals.at[at])
        copy.start()
        copies.append(copy)
    for at in range(steps):
        copies[at].wait()
        rows = slice(at * step, (at + 1) * step)
        total = jnp.zeros((step, lanes), F32)
        for j in range(hidden.shape[1] // lanes):
            part = held[rows, j * lanes:(j + 1) * lanes].astype(F32)
            total += part * part
        inverse = lax.rsqrt(jnp.sum(total, axis=1, keepdims=True) * (1.0 / hidden.shape[1]) + EPS)
        scale[rows, :] = inverse
        columns = (cot[rows, :].astype(F32) * inverse).T.astype(BF16)
        cot_t[:, rows] = columns
        sends[0][:, pl.ds(2 * SWAPS[0] * width + at * step, step)] = columns
        i = 0
        for send, size in zip(sends, SWAPS):
            for j in range(2 * size):
                start = pl.multiple_of((table[i] ^ 1) * width, width)
                send[rows, j * width:(j + 1) * width] = held[rows, pl.ds(start, width)]
                i += 1


def prepare(table, hidden, cot, after, width):
    tokens, features = hidden.shape
    values = cot.shape[1]
    steps = 4
    columns = [2 * size * width for size in SWAPS]
    columns[0] += tokens
    return pl.pallas_call(
        functools.partial(prepare_kernel, width, steps),
        in_specs=[IN_SMEM, IN_HBM, IN_VMEM, ANYWHERE],
        out_specs=[IN_VMEM] * (3 + len(columns)),
        out_shape=[
            jax.ShapeDtypeStruct((tokens, features), BF16),
            jax.ShapeDtypeStruct((tokens, 1), F32),
            jax.ShapeDtypeStruct((values, tokens), BF16),
        ] + [jax.ShapeDtypeStruct((tokens, count), BF16) for count in columns],
        scratch_shapes=[pltpu.SemaphoreType.DMA((steps,))],
        compiler_params=params(LOAD_LIMIT),
        cost_estimate=cost(0, 4 * tokens * features),
    )(table, hidden, cot, after)


def gradient_kernel(base, groups, width, table, hidden, cot_t, *refs):
    visits, outs = refs[:len(SWAPS)], refs[len(SWAPS) + 1:]
    sends = iter(outs[:len(groups)])
    keeps = iter(outs[len(groups):])
    at = base
    for size in groups:
        send = next(sends)
        for j in range(size):
            theirs = swapped(visits, at, width)
            for flip in (1, 0):
                total = jnp.dot(cot_t[...], block(hidden, table[2 * at + flip], width), preferred_element_type=F32)
                total += jnp.dot(
                    visits[0][:, 2 * SWAPS[0] * width:], theirs[:, flip * width:(flip + 1) * width], preferred_element_type=F32
                )
                if flip:
                    send[j] = total.astype(BF16)
                else:
                    next(keeps)[...] = total.astype(BF16)
            at += 1


def gradient(table, hidden, cot_t, visits, after, base, groups, width):
    tokens = hidden.shape[0]
    values = cot_t.shape[0]
    count = sum(groups)
    outs = pl.pallas_call(
        functools.partial(gradient_kernel, base, groups, width),
        in_specs=[IN_SMEM] + [IN_VMEM] * (2 + len(SWAPS)) + [ANYWHERE],
        out_specs=[IN_VMEM] * (len(groups) + count),
        out_shape=[jax.ShapeDtypeStruct((size, values, width), BF16) for size in groups]
        + [jax.ShapeDtypeStruct((values, width), BF16)] * count,
        compiler_params=params(),
        cost_estimate=cost(0, tokens),
    )(table, hidden, cot_t, *visits, after)
    return outs[:len(groups)], outs[len(groups):]


def project_kernel(offsets, sizes, more, extra, width, table, hidden, *refs):
    visits, refs = refs[:len(SWAPS)], refs[len(SWAPS):]
    outs = refs[-3:] if more else refs[-2:]
    start = refs[-5 - extra:-3 - extra] if more else None
    refs = iter(refs)
    weights = [[next(refs) for _ in range(size)] for size in sizes]
    totals = [ref[...] for ref in start] if more else []
    for at in range(0, len(offsets), 2):
        chosen = [OFFSETS.index(off) for off in offsets[at:at + 2]]
        weight = [ref[...].reshape(-1, outs[0].shape[1]) for group in weights[at:at + 2] for ref in group]
        weight = jnp.concatenate(weight, axis=0)
        own = jnp.concatenate([block(hidden, table[2 * i + flip], width) for i in chosen for flip in (0, 1)], axis=1)
        visitors = jnp.concatenate([swapped(visits, i, width) for i in chosen], axis=1)
        products = [jnp.dot(rows, weight, preferred_element_type=F32) for rows in (own, visitors)]
        totals = [t + p for t, p in zip(totals, products)] if totals else products
    outs[0][...] = totals[0]
    if more:
        half = outs[1].shape[0]
        outs[1][...] = totals[1][:half].astype(BF16)
        outs[2][...] = totals[1][half:].astype(BF16)
    else:
        outs[1][...] = totals[1]


def project(table, hidden, visits, weights, start, after, width):
    tokens = hidden.shape[0]
    arrays = [w for group in weights.values() for w in group]
    values = arrays[0].shape[-1]
    size = sum(w.size for w in arrays)
    more = [] if start is None else list(start)
    whole = jax.ShapeDtypeStruct((tokens, values), F32)
    half = jax.ShapeDtypeStruct((tokens // 2, values), BF16)
    out_shape = [whole, half, half] if more else [whole, whole]
    return pl.pallas_call(
        functools.partial(project_kernel, tuple(weights), [len(g) for g in weights.values()], bool(more), len(after), width),
        in_specs=[IN_SMEM] + [IN_VMEM] * (1 + len(SWAPS) + len(arrays) + len(more)) + [ANYWHERE] * len(after),
        out_specs=[IN_VMEM] * len(out_shape),
        out_shape=out_shape,
        compiler_params=params(),
        cost_estimate=cost(4 * tokens * size, 0),
    )(table, hidden, *visits, *arrays, *more, *after)


def small(kernel, inputs, after, shapes, dtype=BF16):
    def body(*refs):
        kernel(*refs[:len(inputs)], *refs[len(inputs) + len(after):])

    return pl.pallas_call(
        body,
        in_specs=[IN_VMEM] * len(inputs) + [ANYWHERE] * len(after),
        out_specs=[IN_VMEM] * len(shapes),
        out_shape=[jax.ShapeDtypeStruct(shape, dtype) for shape in shapes],
        compiler_params=params(),
        cost_estimate=cost(0, inputs[0].shape[0]),
    )(*inputs, *after)


def tie(arrays, after):
    count = len(arrays)
    return pl.pallas_call(
        lambda *refs: None,
        in_specs=[ANYWHERE] * (count + len(after)),
        out_specs=[ANYWHERE] * count,
        out_shape=[jax.ShapeDtypeStruct(a.shape, a.dtype) for a in arrays],
        input_output_aliases={i: i for i in range(count)},
        compiler_params=params(),
        cost_estimate=cost(0, 1),
    )(*arrays, *after)


def pair(one, other, after):
    def kernel(one, other, out):
        out[0] = one[...]
        out[1] = other[...]

    return small(kernel, [one, other], after, [(2, *one.shape)])[0]


def split(pair_up, pair_down, after):
    def kernel(up, down, out_up, out_down):
        out_up[...] = up[0]
        out_down[...] = down[1]

    return small(kernel, [pair_up, pair_down], after, [pair_up.shape[1:]] * 2)


def total_of(terms, rows=slice(None)):
    return sum(t[rows].astype(F32) for t in terms).astype(BF16)


def begin(terms, places, after):
    values, width = terms[0].shape
    half = values // 2

    def kernel(keep, arrived, upper, lower):
        parts = (keep, arrived.at[places[0]])
        upper[...] = total_of(parts, slice(0, half))
        lower[...] = total_of(parts, slice(half, values))

    return small(kernel, terms, after, [(half, width)] * 2)


def carry(ups, downs, places, after):
    values, width = ups[0].shape

    def kernel(keep_up, arrived_up, up, keep_down, arrived_down, down, out_up, out_down):
        up_parts = (keep_up, arrived_up.at[places[0]])
        down_parts = (keep_down, arrived_down.at[places[1]])
        if up.shape[0] == values:
            out_up[...] = total_of((*up_parts, up))
            out_down[...] = total_of((*down_parts, down))
        else:
            half = values // 2
            upper, lower = slice(0, half), slice(half, values)
            out_up[upper, :] = (sum(t[upper].astype(F32) for t in up_parts) + up[...].astype(F32)).astype(BF16)
            out_up[lower, :] = total_of(up_parts, lower)
            out_down[upper, :] = total_of(down_parts, upper)
            out_down[lower, :] = (sum(t[lower].astype(F32) for t in down_parts) + down[...].astype(F32)).astype(BF16)

    return small(kernel, [*ups, *downs], after, [(values, width)] * 2)


def end(terms, place, after):
    def kernel(keep, arrived, up, down, out):
        out[...] = total_of((keep, arrived.at[place], up, down))

    return small(kernel, terms, after, [terms[0].shape])[0]


def scaled_values(product, upper, lower, scale):
    def kernel(product, upper, lower, scale, out):
        half = upper.shape[0]
        for arrived, rows in ((upper, slice(0, half)), (lower, slice(half, 2 * half))):
            out[rows, :] = ((product[rows, :] + arrived[...].astype(F32)) * scale[rows, :]).astype(BF16)

    return small(kernel, [product, upper, lower, scale], [], [product.shape])[0]


def diagonal(width):
    return lax.broadcasted_iota(jnp.int32, (width, width), 0) == lax.broadcasted_iota(jnp.int32, (width, width), 1)


def as_column(row):
    return jnp.sum(jnp.where(diagonal(row.shape[1]), row, 0.0), axis=1, keepdims=True)


def as_row(column):
    return jnp.sum(jnp.where(diagonal(column.shape[0]), column, 0.0), axis=0, keepdims=True)


def scale_kernel(gain, weight, out):
    out[...] = (weight[0].astype(F32) * as_column(gain[...].astype(F32))).astype(BF16)


def scale_weight(gain, weight):
    return pl.pallas_call(scale_kernel, out_shape=jax.ShapeDtypeStruct(weight.shape[1:], BF16), compiler_params=params())(gain, weight)


def finish_kernel(total, gain, weight, grad_weight_in, grad_gain_in, grad_weight, grad_gain):
    summed = total[...].astype(F32).T
    grad_weight[0] = grad_weight_in[0] + as_column(gain[...].astype(F32)) * summed
    grad_gain[...] = grad_gain_in[...] + as_row(jnp.sum(weight[0].astype(F32) * summed, axis=1, keepdims=True))


def finish(total, gain, weight, grad_weight_in, grad_gain_in):
    return pl.pallas_call(
        finish_kernel,
        out_shape=[jax.ShapeDtypeStruct(a.shape, F32) for a in (grad_weight_in, grad_gain_in)],
        compiler_params=params(),
    )(total, gain, weight, grad_weight_in, grad_gain_in)


def per_device(hidden, gain, value_weight, cotangent, grad_weight_in, grad_gain_in):
    width = value_weight.shape[1]
    x, z, core = (lax.axis_index(a) for a in ("x", "z", "core"))
    table = jnp.stack(
        [fsdp_index(x ^ flip, (z + off + NZ) % NZ, core) for off in OFFSETS for flip in (0, 1)]
    ).astype(jnp.int32)

    scaled_weight = scale_weight(gain, value_weight)
    layer = [along_blk(scaled_weight, 1, flip) for flip in (0, 1)]

    held, scale, cot_t, *sends = prepare(table, hidden, cotangent, scaled_weight, width)
    visits = [swap_core(send) for send in sends]

    early = [visits[0]] * len(SWAPS)
    sends_1, keeps_1 = gradient(table, held, cot_t, early, cot_t, 0, GROUPS[0], width)
    sends_2, keeps_2 = gradient(table, held, cot_t, visits, sends_1[-1], FIRST, GROUPS[1], width)
    arrived = [swap_x(send) for send in (*sends_1, *sends_2)]
    keeps = [*keeps_1, *keeps_2]
    places = [(i, j) for i, size in enumerate(GROUPS[0] + GROUPS[1]) for j in range(size)]
    mine = {off: (keeps[i], arrived[places[i][0]]) for i, off in enumerate(OFFSETS)}
    place = {off: places[i][1] for i, off in enumerate(OFFSETS)}

    layer = pair(*layer, [sends_1[-1]])
    up, down = begin(mine[4], (place[4],), [sends_2[-1]])
    weights = {0: [layer]}
    layer_up = layer_down = layer
    for step in (1, 2, 3):
        layer_up, layer_down = along_z(layer_up, 1), along_z(layer_down, -1)
        if step < 3:
            layer_up, layer_down = tie([layer_up, layer_down], [up, down, mine[4 - step][1]])
        else:
            far_up, far_down = split(layer_up, layer_down, [up, down, mine[1][1]])
        weights[-step], weights[step] = [layer_up], [layer_down]
        off = 4 - step
        up, down = along_z(up, 1), along_z(down, -1)
        ready = [layer_up, layer_down] if step < 3 else [mine[0][1]]
        up, down = carry((*mine[off], up), (*mine[-off], down), (place[off], place[-off]), ready)
    weights[4] = [along_z(far_up, 1), along_z(far_down, -1)]

    near = {off: weights[off] for off in (0, -1, 1, -2, 2)}
    far = {off: weights[off] for off in (-3, 3, 4)}
    products = project(table, held, visits, near, None, [up], width)
    product, *products = project(table, held, visits, far, products, [], width)
    up, down = along_z(up, 1), along_z(down, -1)
    total = along_blk(end((*mine[0], up, down), place[0], []), -1, 0)
    values = scaled_values(product, *(swap_core(p) for p in products), scale)

    return values, *finish(total, gain, value_weight, grad_weight_in, grad_gain_in)


def solution(mesh):
    fsdp = ("x", "z", "core")
    return jax.shard_map(
        per_device,
        mesh=Mesh(mesh.devices.reshape(NB, NX, NZ, NC), ("blk", *fsdp)),
        in_specs=(
            P(("blk", *fsdp), None),
            P("blk", fsdp),
            P("blk", fsdp, None),
            P(("blk", *fsdp), None),
            P("blk", fsdp, None),
            P("blk", fsdp),
        ),
        out_specs=(P(("blk", *fsdp), None), P("blk", fsdp, None), P("blk", fsdp)),
        check_vma=False,
    )
```

```python
import functools

import jax
import jax.numpy as jnp
from jax import lax
from jax.experimental import pallas as pl
from jax.experimental.pallas import tpu as pltpu
from jax.sharding import Mesh, PartitionSpec as P

NX, NZ, NC = 2, 8, 2
NB = 8
EPS = 1e-05
BF16 = jnp.bfloat16
F32 = jnp.float32
OFFSETS = (4, 3, -3, 2, -2, 1, -1, 0)
GROUPS = ((1, 2), (2, 2, 1))
FIRST = sum(GROUPS[0])
SWAPS = (3, 2, 3)
VMEM_LIMIT = 16 * 1024 * 1024
LOAD_LIMIT = 36 * 1024 * 1024


def fsdp_index(x, z, core):
    return (x * NZ + z) * NC + core


def move(value, change):
    pairs = [
        (fsdp_index(x, z, c), fsdp_index(*change(x, z, c)))
        for x in range(NX)
        for z in range(NZ)
        for c in range(NC)
    ]
    return lax.ppermute(value, ("x", "z", "core"), pairs)


def along_z(value, steps):
    return move(value, lambda x, z, c: (x, (z + steps) % NZ, c))


def swap_x(value):
    return move(value, lambda x, z, c: (1 - x, z, c))


def swap_core(value):
    return move(value, lambda x, z, c: (x, z, 1 - c))


def along_blk(value, steps, flip_x):
    size = NX * NZ * NC
    pairs = [
        (b * size + fsdp_index(x, z, c), ((b + steps) % NB) * size + fsdp_index(x ^ flip_x, z, c))
        for b in range(NB)
        for x in range(NX)
        for z in range(NZ)
        for c in range(NC)
    ]
    return lax.ppermute(value, ("blk", "x", "z", "core"), pairs)


def params(limit=VMEM_LIMIT):
    return pltpu.CompilerParams(vmem_limit_bytes=limit)


def cost(flops, size):
    return pl.CostEstimate(flops=flops, bytes_accessed=size, transcendentals=0)


IN_VMEM = pl.BlockSpec(memory_space=pltpu.VMEM)
IN_SMEM = pl.BlockSpec(memory_space=pltpu.SMEM)
ANYWHERE = pl.BlockSpec(memory_space=pl.ANY)
IN_HBM = pl.BlockSpec(memory_space=pltpu.HBM)


def block(ref, index, width):
    return ref[:, pl.ds(pl.multiple_of(index * width, width), width)]


def swapped(visits, index, width):
    for visit, size in zip(visits, SWAPS):
        if index < size:
            return visit[:, 2 * index * width:2 * (index + 1) * width]
        index -= size


def prepare_kernel(width, steps, table, hidden, cot, after, held, scale, cot_t, *rest):
    sends, arrivals = rest[:-1], rest[-1]
    step = hidden.shape[0] // steps
    lanes = 128
    copies = []
    for at in range(steps):
        rows = pl.ds(at * step, step)
        copy = pltpu.make_async_copy(hidden.at[rows, :], held.at[rows, :], arrivals.at[at])
        copy.start()
        copies.append(copy)
    for at in range(steps):
        copies[at].wait()
        rows = slice(at * step, (at + 1) * step)
        total = jnp.zeros((step, lanes), F32)
        for j in range(hidden.shape[1] // lanes):
            part = held[rows, j * lanes:(j + 1) * lanes].astype(F32)
            total += part * part
        inverse = lax.rsqrt(jnp.sum(total, axis=1, keepdims=True) * (1.0 / hidden.shape[1]) + EPS)
        scale[rows, :] = inverse
        columns = (cot[rows, :].astype(F32) * inverse).T.astype(BF16)
        cot_t[:, rows] = columns
        sends[0][:, pl.ds(2 * SWAPS[0] * width + at * step, step)] = columns
        i = 0
        for send, size in zip(sends, SWAPS):
            for j in range(2 * size):
                start = pl.multiple_of((table[i] ^ 1) * width, width)
                send[rows, j * width:(j + 1) * width] = held[rows, pl.ds(start, width)]
                i += 1


def prepare(table, hidden, cot, after, width):
    tokens, features = hidden.shape
    values = cot.shape[1]
    steps = 4
    columns = [2 * size * width for size in SWAPS]
    columns[0] += tokens
    return pl.pallas_call(
        functools.partial(prepare_kernel, width, steps),
        in_specs=[IN_SMEM, IN_HBM, IN_VMEM, ANYWHERE],
        out_specs=[IN_VMEM] * (3 + len(columns)),
        out_shape=[
            jax.ShapeDtypeStruct((tokens, features), BF16),
            jax.ShapeDtypeStruct((tokens, 1), F32),
            jax.ShapeDtypeStruct((values, tokens), BF16),
        ] + [jax.ShapeDtypeStruct((tokens, count), BF16) for count in columns],
        scratch_shapes=[pltpu.SemaphoreType.DMA((steps,))],
        compiler_params=params(LOAD_LIMIT),
        cost_estimate=cost(0, 4 * tokens * features),
    )(table, hidden, cot, after)


def gradient_kernel(base, groups, width, table, hidden, cot_t, *refs):
    visits, outs = refs[:len(SWAPS)], refs[len(SWAPS) + 1:]
    sends = iter(outs[:len(groups)])
    keeps = iter(outs[len(groups):])
    at = base
    for size in groups:
        send = next(sends)
        for j in range(size):
            theirs = swapped(visits, at, width)
            for flip in (1, 0):
                total = jnp.dot(cot_t[...], block(hidden, table[2 * at + flip], width), preferred_element_type=F32)
                total += jnp.dot(
                    visits[0][:, 2 * SWAPS[0] * width:], theirs[:, flip * width:(flip + 1) * width], preferred_element_type=F32
                )
                if flip:
                    send[j] = total.astype(BF16)
                else:
                    next(keeps)[...] = total.astype(BF16)
            at += 1


def gradient(table, hidden, cot_t, visits, after, base, groups, width):
    tokens = hidden.shape[0]
    values = cot_t.shape[0]
    count = sum(groups)
    outs = pl.pallas_call(
        functools.partial(gradient_kernel, base, groups, width),
        in_specs=[IN_SMEM] + [IN_VMEM] * (2 + len(SWAPS)) + [ANYWHERE],
        out_specs=[IN_VMEM] * (len(groups) + count),
        out_shape=[jax.ShapeDtypeStruct((size, values, width), BF16) for size in groups]
        + [jax.ShapeDtypeStruct((values, width), BF16)] * count,
        compiler_params=params(),
        cost_estimate=cost(0, tokens),
    )(table, hidden, cot_t, *visits, after)
    return outs[:len(groups)], outs[len(groups):]


def project_kernel(offsets, sizes, more, extra, width, table, hidden, *refs):
    visits, refs = refs[:len(SWAPS)], refs[len(SWAPS):]
    outs = refs[-3:] if more else refs[-2:]
    start = refs[-5 - extra:-3 - extra] if more else None
    refs = iter(refs)
    weights = [[next(refs) for _ in range(size)] for size in sizes]
    totals = [ref[...] for ref in start] if more else []
    for at in range(0, len(offsets), 2):
        chosen = [OFFSETS.index(off) for off in offsets[at:at + 2]]
        weight = [ref[...].reshape(-1, outs[0].shape[1]) for group in weights[at:at + 2] for ref in group]
        weight = jnp.concatenate(weight, axis=0)
        own = jnp.concatenate([block(hidden, table[2 * i + flip], width) for i in chosen for flip in (0, 1)], axis=1)
        visitors = jnp.concatenate([swapped(visits, i, width) for i in chosen], axis=1)
        products = [jnp.dot(rows, weight, preferred_element_type=F32) for rows in (own, visitors)]
        totals = [t + p for t, p in zip(totals, products)] if totals else products
    outs[0][...] = totals[0]
    if more:
        half = outs[1].shape[0]
        outs[1][...] = totals[1][:half].astype(BF16)
        outs[2][...] = totals[1][half:].astype(BF16)
    else:
        outs[1][...] = totals[1]


def project(table, hidden, visits, weights, start, after, width):
    tokens = hidden.shape[0]
    arrays = [w for group in weights.values() for w in group]
    values = arrays[0].shape[-1]
    size = sum(w.size for w in arrays)
    more = [] if start is None else list(start)
    whole = jax.ShapeDtypeStruct((tokens, values), F32)
    half = jax.ShapeDtypeStruct((tokens // 2, values), BF16)
    out_shape = [whole, half, half] if more else [whole, whole]
    return pl.pallas_call(
        functools.partial(project_kernel, tuple(weights), [len(g) for g in weights.values()], bool(more), len(after), width),
        in_specs=[IN_SMEM] + [IN_VMEM] * (1 + len(SWAPS) + len(arrays) + len(more)) + [ANYWHERE] * len(after),
        out_specs=[IN_VMEM] * len(out_shape),
        out_shape=out_shape,
        compiler_params=params(),
        cost_estimate=cost(4 * tokens * size, 0),
    )(table, hidden, *visits, *arrays, *more, *after)


def small(kernel, inputs, after, shapes, dtype=BF16):
    def body(*refs):
        kernel(*refs[:len(inputs)], *refs[len(inputs) + len(after):])

    return pl.pallas_call(
        body,
        in_specs=[IN_VMEM] * len(inputs) + [ANYWHERE] * len(after),
        out_specs=[IN_VMEM] * len(shapes),
        out_shape=[jax.ShapeDtypeStruct(shape, dtype) for shape in shapes],
        compiler_params=params(),
        cost_estimate=cost(0, inputs[0].shape[0]),
    )(*inputs, *after)


def tie(arrays, after):
    count = len(arrays)
    return pl.pallas_call(
        lambda *refs: None,
        in_specs=[ANYWHERE] * (count + len(after)),
        out_specs=[ANYWHERE] * count,
        out_shape=[jax.ShapeDtypeStruct(a.shape, a.dtype) for a in arrays],
        input_output_aliases={i: i for i in range(count)},
        compiler_params=params(),
        cost_estimate=cost(0, 1),
    )(*arrays, *after)


def pair(one, other, after):
    def kernel(one, other, out):
        out[0] = one[...]
        out[1] = other[...]

    return small(kernel, [one, other], after, [(2, *one.shape)])[0]


def split(pair_up, pair_down, after):
    def kernel(up, down, out_up, out_down):
        out_up[...] = up[0]
        out_down[...] = down[1]

    return small(kernel, [pair_up, pair_down], after, [pair_up.shape[1:]] * 2)


def total_of(terms, rows=slice(None)):
    return sum(t[rows].astype(F32) for t in terms).astype(BF16)


def begin(terms, places, after):
    values, width = terms[0].shape
    half = values // 2

    def kernel(keep, arrived, upper, lower):
        parts = (keep, arrived.at[places[0]])
        upper[...] = total_of(parts, slice(0, half))
        lower[...] = total_of(parts, slice(half, values))

    return small(kernel, terms, after, [(half, width)] * 2)


def carry(ups, downs, places, after):
    values, width = ups[0].shape

    def kernel(keep_up, arrived_up, up, keep_down, arrived_down, down, out_up, out_down):
        up_parts = (keep_up, arrived_up.at[places[0]])
        down_parts = (keep_down, arrived_down.at[places[1]])
        if up.shape[0] == values:
            out_up[...] = total_of((*up_parts, up))
            out_down[...] = total_of((*down_parts, down))
        else:
            half = values // 2
            upper, lower = slice(0, half), slice(half, values)
            out_up[upper, :] = (sum(t[upper].astype(F32) for t in up_parts) + up[...].astype(F32)).astype(BF16)
            out_up[lower, :] = total_of(up_parts, lower)
            out_down[upper, :] = total_of(down_parts, upper)
            out_down[lower, :] = (sum(t[lower].astype(F32) for t in down_parts) + down[...].astype(F32)).astype(BF16)

    return small(kernel, [*ups, *downs], after, [(values, width)] * 2)


def end(terms, place, after):
    def kernel(keep, arrived, up, down, out):
        out[...] = total_of((keep, arrived.at[place], up, down))

    return small(kernel, terms, after, [terms[0].shape])[0]


def scaled_values(product, upper, lower, scale):
    def kernel(product, upper, lower, scale, out):
        half = upper.shape[0]
        for arrived, rows in ((upper, slice(0, half)), (lower, slice(half, 2 * half))):
            out[rows, :] = ((product[rows, :] + arrived[...].astype(F32)) * scale[rows, :]).astype(BF16)

    return small(kernel, [product, upper, lower, scale], [], [product.shape])[0]


def diagonal(width):
    return lax.broadcasted_iota(jnp.int32, (width, width), 0) == lax.broadcasted_iota(jnp.int32, (width, width), 1)


def as_column(row):
    return jnp.sum(jnp.where(diagonal(row.shape[1]), row, 0.0), axis=1, keepdims=True)


def as_row(column):
    return jnp.sum(jnp.where(diagonal(column.shape[0]), column, 0.0), axis=0, keepdims=True)


def scale_kernel(gain, weight, out):
    out[...] = (weight[0].astype(F32) * as_column(gain[...].astype(F32))).astype(BF16)


def scale_weight(gain, weight):
    return pl.pallas_call(scale_kernel, out_shape=jax.ShapeDtypeStruct(weight.shape[1:], BF16), compiler_params=params())(gain, weight)


def finish_kernel(total, gain, weight, grad_weight_in, grad_gain_in, grad_weight, grad_gain):
    summed = total[...].astype(F32).T
    grad_weight[0] = grad_weight_in[0] + as_column(gain[...].astype(F32)) * summed
    grad_gain[...] = grad_gain_in[...] + as_row(jnp.sum(weight[0].astype(F32) * summed, axis=1, keepdims=True))


def finish(total, gain, weight, grad_weight_in, grad_gain_in):
    return pl.pallas_call(
        finish_kernel,
        out_shape=[jax.ShapeDtypeStruct(a.shape, F32) for a in (grad_weight_in, grad_gain_in)],
        compiler_params=params(),
    )(total, gain, weight, grad_weight_in, grad_gain_in)


def per_device(hidden, gain, value_weight, cotangent, grad_weight_in, grad_gain_in):
    width = value_weight.shape[1]
    x, z, core = (lax.axis_index(a) for a in ("x", "z", "core"))
    table = jnp.stack(
        [fsdp_index(x ^ flip, (z + off + NZ) % NZ, core) for off in OFFSETS for flip in (0, 1)]
    ).astype(jnp.int32)

    scaled_weight = scale_weight(gain, value_weight)
    layer = [along_blk(scaled_weight, 1, flip) for flip in (0, 1)]

    held, scale, cot_t, *sends = prepare(table, hidden, cotangent, scaled_weight, width)
    visits = [swap_core(send) for send in sends]

    early = [visits[0]] * len(SWAPS)
    sends_1, keeps_1 = gradient(table, held, cot_t, early, cot_t, 0, GROUPS[0], width)
    sends_2, keeps_2 = gradient(table, held, cot_t, visits, sends_1[-1], FIRST, GROUPS[1], width)
    arrived = [swap_x(send) for send in (*sends_1, *sends_2)]
    keeps = [*keeps_1, *keeps_2]
    places = [(i, j) for i, size in enumerate(GROUPS[0] + GROUPS[1]) for j in range(size)]
    mine = {off: (keeps[i], arrived[places[i][0]]) for i, off in enumerate(OFFSETS)}
    place = {off: places[i][1] for i, off in enumerate(OFFSETS)}

    layer = pair(*layer, [arrived[0]])
    up, down = begin(mine[4], (place[4],), [])
    weights = {0: [layer]}
    layer_up = layer_down = layer
    for step in (1, 2, 3):
        layer_up, layer_down = along_z(layer_up, 1), along_z(layer_down, -1)
        off = 4 - step
        up, down = along_z(up, 1), along_z(down, -1)
        ready = [mine[0][1]] if step == 3 else []
        up, down = carry((*mine[off], up), (*mine[-off], down), (place[off], place[-off]), ready)
        if step < 3:
            layer_up, layer_down = tie([layer_up, layer_down], [up, down])
        else:
            far_up, far_down = split(layer_up, layer_down, [up, down])
        weights[-step], weights[step] = [layer_up], [layer_down]
    weights[4] = [along_z(far_up, 1), along_z(far_down, -1)]

    near = {off: weights[off] for off in (0, -1, 1, -2, 2)}
    far = {off: weights[off] for off in (-3, 3, 4)}
    products = project(table, held, visits, near, None, [up], width)
    product, *products = project(table, held, visits, far, products, [], width)
    up, down = along_z(up, 1), along_z(down, -1)
    total = along_blk(end((*mine[0], up, down), place[0], []), -1, 0)
    values = scaled_values(product, *(swap_core(p) for p in products), scale)

    return values, *finish(total, gain, value_weight, grad_weight_in, grad_gain_in)


def solution(mesh):
    fsdp = ("x", "z", "core")
    return jax.shard_map(
        per_device,
        mesh=Mesh(mesh.devices.reshape(NB, NX, NZ, NC), ("blk", *fsdp)),
        in_specs=(
            P(("blk", *fsdp), None),
            P("blk", fsdp),
            P("blk", fsdp, None),
            P(("blk", *fsdp), None),
            P("blk", fsdp, None),
            P("blk", fsdp),
        ),
        out_specs=(P(("blk", *fsdp), None), P("blk", fsdp, None), P("blk", fsdp)),
        check_vma=False,
    )
```

```python
import functools

import jax
import jax.numpy as jnp
from jax import lax
from jax.experimental import pallas as pl
from jax.experimental.pallas import tpu as pltpu
from jax.sharding import Mesh, PartitionSpec as P

NX, NZ, NC = 2, 8, 2
NB = 8
EPS = 1e-05
BF16 = jnp.bfloat16
F32 = jnp.float32
OFFSETS = (4, 3, -3, 2, -2, 1, -1, 0)
GROUPS = ((1,), (2, 2, 2, 1))
FIRST = sum(GROUPS[0])
SWAPS = (2, 2, 2, 2)
VMEM_LIMIT = 16 * 1024 * 1024
LOAD_LIMIT = 36 * 1024 * 1024


def fsdp_index(x, z, core):
    return (x * NZ + z) * NC + core


def move(value, change):
    pairs = [
        (fsdp_index(x, z, c), fsdp_index(*change(x, z, c)))
        for x in range(NX)
        for z in range(NZ)
        for c in range(NC)
    ]
    return lax.ppermute(value, ("x", "z", "core"), pairs)


def along_z(value, steps):
    return move(value, lambda x, z, c: (x, (z + steps) % NZ, c))


def swap_x(value):
    return move(value, lambda x, z, c: (1 - x, z, c))


def swap_core(value):
    return move(value, lambda x, z, c: (x, z, 1 - c))


def along_blk(value, steps, flip_x):
    size = NX * NZ * NC
    pairs = [
        (b * size + fsdp_index(x, z, c), ((b + steps) % NB) * size + fsdp_index(x ^ flip_x, z, c))
        for b in range(NB)
        for x in range(NX)
        for z in range(NZ)
        for c in range(NC)
    ]
    return lax.ppermute(value, ("blk", "x", "z", "core"), pairs)


def params(limit=VMEM_LIMIT):
    return pltpu.CompilerParams(vmem_limit_bytes=limit)


def cost(flops, size):
    return pl.CostEstimate(flops=flops, bytes_accessed=size, transcendentals=0)


IN_VMEM = pl.BlockSpec(memory_space=pltpu.VMEM)
IN_SMEM = pl.BlockSpec(memory_space=pltpu.SMEM)
ANYWHERE = pl.BlockSpec(memory_space=pl.ANY)
IN_HBM = pl.BlockSpec(memory_space=pltpu.HBM)


def block(ref, index, width):
    return ref[:, pl.ds(pl.multiple_of(index * width, width), width)]


def swapped(visits, index, width):
    for visit, size in zip(visits, SWAPS):
        if index < size:
            return visit[:, 2 * index * width:2 * (index + 1) * width]
        index -= size


def prepare_kernel(width, steps, table, hidden, cot, after, held, scale, cot_t, *rest):
    sends, arrivals = rest[:-1], rest[-1]
    step = hidden.shape[0] // steps
    lanes = 128
    copies = []
    for at in range(steps):
        rows = pl.ds(at * step, step)
        copy = pltpu.make_async_copy(hidden.at[rows, :], held.at[rows, :], arrivals.at[at])
        copy.start()
        copies.append(copy)
    for at in range(steps):
        copies[at].wait()
        rows = slice(at * step, (at + 1) * step)
        total = jnp.zeros((step, lanes), F32)
        for j in range(hidden.shape[1] // lanes):
            part = held[rows, j * lanes:(j + 1) * lanes].astype(F32)
            total += part * part
        inverse = lax.rsqrt(jnp.sum(total, axis=1, keepdims=True) * (1.0 / hidden.shape[1]) + EPS)
        scale[rows, :] = inverse
        columns = (cot[rows, :].astype(F32) * inverse).T.astype(BF16)
        cot_t[:, rows] = columns
        sends[0][:, pl.ds(2 * SWAPS[0] * width + at * step, step)] = columns
        i = 0
        for send, size in zip(sends, SWAPS):
            for j in range(2 * size):
                start = pl.multiple_of((table[i] ^ 1) * width, width)
                send[rows, j * width:(j + 1) * width] = held[rows, pl.ds(start, width)]
                i += 1


def prepare(table, hidden, cot, after, width):
    tokens, features = hidden.shape
    values = cot.shape[1]
    steps = 4
    columns = [2 * size * width for size in SWAPS]
    columns[0] += tokens
    return pl.pallas_call(
        functools.partial(prepare_kernel, width, steps),
        in_specs=[IN_SMEM, IN_HBM, IN_VMEM, ANYWHERE],
        out_specs=[IN_VMEM] * (3 + len(columns)),
        out_shape=[
            jax.ShapeDtypeStruct((tokens, features), BF16),
            jax.ShapeDtypeStruct((tokens, 1), F32),
            jax.ShapeDtypeStruct((values, tokens), BF16),
        ] + [jax.ShapeDtypeStruct((tokens, count), BF16) for count in columns],
        scratch_shapes=[pltpu.SemaphoreType.DMA((steps,))],
        compiler_params=params(LOAD_LIMIT),
        cost_estimate=cost(0, 4 * tokens * features),
    )(table, hidden, cot, after)


def gradient_kernel(base, groups, width, table, hidden, cot_t, *refs):
    visits, outs = refs[:len(SWAPS)], refs[len(SWAPS) + 1:]
    sends = iter(outs[:len(groups)])
    keeps = iter(outs[len(groups):])
    at = base
    for size in groups:
        send = next(sends)
        for j in range(size):
            theirs = swapped(visits, at, width)
            for flip in (1, 0):
                total = jnp.dot(cot_t[...], block(hidden, table[2 * at + flip], width), preferred_element_type=F32)
                total += jnp.dot(
                    visits[0][:, 2 * SWAPS[0] * width:], theirs[:, flip * width:(flip + 1) * width], preferred_element_type=F32
                )
                half = total.shape[0] // 2
                total = jnp.concatenate([total[:half], total[half:]], axis=1).astype(BF16)
                if flip:
                    send[j] = total
                else:
                    next(keeps)[...] = total
            at += 1


def gradient(table, hidden, cot_t, visits, after, base, groups, width):
    tokens = hidden.shape[0]
    values = cot_t.shape[0]
    count = sum(groups)
    outs = pl.pallas_call(
        functools.partial(gradient_kernel, base, groups, width),
        in_specs=[IN_SMEM] + [IN_VMEM] * (2 + len(SWAPS)) + [ANYWHERE],
        out_specs=[IN_VMEM] * (len(groups) + count),
        out_shape=[jax.ShapeDtypeStruct((size, values // 2, 2 * width), BF16) for size in groups]
        + [jax.ShapeDtypeStruct((values // 2, 2 * width), BF16)] * count,
        compiler_params=params(),
        cost_estimate=cost(0, tokens),
    )(table, hidden, cot_t, *visits, after)
    return outs[:len(groups)], outs[len(groups):]


def project_kernel(offsets, rows, more, extra, width, table, hidden, *refs):
    visits, refs = refs[:len(SWAPS)], refs[len(SWAPS):]
    outs = refs[-3:] if more else refs[-2:]
    start = refs[-5 - extra:-3 - extra] if more else None
    refs = iter(refs)
    weights = [[next(refs)[:count] for count in group] for group in rows]
    totals = [ref[...] for ref in start] if more else []
    for at in range(0, len(offsets), 2):
        chosen = [OFFSETS.index(off) for off in offsets[at:at + 2]]
        weight = jnp.concatenate([part for group in weights[at:at + 2] for part in group], axis=0)
        own = jnp.concatenate([block(hidden, table[2 * i + flip], width) for i in chosen for flip in (0, 1)], axis=1)
        visitors = jnp.concatenate([swapped(visits, i, width) for i in chosen], axis=1)
        products = [jnp.dot(rows, weight, preferred_element_type=F32) for rows in (own, visitors)]
        totals = [t + p for t, p in zip(totals, products)] if totals else products
    outs[0][...] = totals[0]
    if more:
        half = outs[1].shape[0]
        outs[1][...] = totals[1][:half].astype(BF16)
        outs[2][...] = totals[1][half:].astype(BF16)
    else:
        outs[1][...] = totals[1]


def project(table, hidden, visits, weights, start, after, width):
    tokens = hidden.shape[0]
    arrays = [w for group in weights.values() for w, _ in group]
    rows = [[count for _, count in group] for group in weights.values()]
    values = arrays[0].shape[-1]
    size = values * sum(map(sum, rows))
    more = [] if start is None else list(start)
    whole = jax.ShapeDtypeStruct((tokens, values), F32)
    half = jax.ShapeDtypeStruct((tokens // 2, values), BF16)
    out_shape = [whole, half, half] if more else [whole, whole]
    return pl.pallas_call(
        functools.partial(project_kernel, tuple(weights), rows, bool(more), len(after), width),
        in_specs=[IN_SMEM] + [IN_VMEM] * (1 + len(SWAPS) + len(arrays) + len(more)) + [ANYWHERE] * len(after),
        out_specs=[IN_VMEM] * len(out_shape),
        out_shape=out_shape,
        compiler_params=params(),
        cost_estimate=cost(4 * tokens * size, 0),
    )(table, hidden, *visits, *arrays, *more, *after)


def small(kernel, inputs, after, shapes, dtype=BF16):
    def body(*refs):
        kernel(*refs[:len(inputs)], *refs[len(inputs) + len(after):])

    return pl.pallas_call(
        body,
        in_specs=[IN_VMEM] * len(inputs) + [ANYWHERE] * len(after),
        out_specs=[IN_VMEM] * len(shapes),
        out_shape=[jax.ShapeDtypeStruct(shape, dtype) for shape in shapes],
        compiler_params=params(),
        cost_estimate=cost(0, inputs[0].shape[0]),
    )(*inputs, *after)


def tie(arrays, after):
    count = len(arrays)
    return pl.pallas_call(
        lambda *refs: None,
        in_specs=[ANYWHERE] * (count + len(after)),
        out_specs=[ANYWHERE] * count,
        out_shape=[jax.ShapeDtypeStruct(a.shape, a.dtype) for a in arrays],
        input_output_aliases={i: i for i in range(count)},
        compiler_params=params(),
        cost_estimate=cost(0, 1),
    )(*arrays, *after)


def summed(terms):
    return sum(t.astype(F32) for t in terms).astype(BF16)


def begin(layer, far, ring, after):
    keep, arrived, place = far
    width, values = layer.shape
    part = width // 4

    def kernel(layer, keep, arrived, up, down):
        for i, out in enumerate((up, down)):
            rows = slice((2 * ring + i) * part, (2 * ring + i + 1) * part)
            out[:width] = layer[...]
            out[width:] = summed((keep[rows], arrived[place, rows]))

    return small(kernel, [layer, keep, arrived], after, [(width + part, values)] * 2)


def advance(up, down, above, below, ring, width, step, after):
    values = up.shape[1]
    half = width // 2
    rows = slice(ring * half, (ring + 1) * half)
    layer_rows = half if step == 3 else width

    def kernel(up, keep_up, arrived_up, down, keep_down, arrived_down, next_up, next_down):
        next_up[:layer_rows] = up[:layer_rows]
        next_down[:layer_rows] = down[width - layer_rows:width]
        mine_up = keep_up[rows].astype(F32) + arrived_up[above[2], rows].astype(F32)
        mine_down = keep_down[rows].astype(F32) + arrived_down[below[2], rows].astype(F32)
        came_up, came_down = up[width:].astype(F32), down[width:].astype(F32)
        if step == 1:
            part = half // 2
            mine_up = jnp.concatenate([mine_up[:part] + came_up, mine_up[part:]], axis=0)
            mine_down = jnp.concatenate([mine_down[:part], mine_down[part:] + came_down], axis=0)
        else:
            mine_up += came_up
            mine_down += came_down
        next_up[layer_rows:] = mine_up.astype(BF16)
        next_down[layer_rows:] = mine_down.astype(BF16)

    return small(kernel, [up, *above[:2], down, *below[:2]], after, [(layer_rows + half, values)] * 2)


def end(rings, own):
    keep, arrived, place = own
    half = keep.shape[0] // 2

    def kernel(keep, arrived, *refs):
        loads, out = refs[:-1], refs[-1]
        for ring in (0, 1):
            rows = slice(ring * half, (ring + 1) * half)
            out[rows] = summed((keep[rows], arrived[place, rows], *(load[half:] for load in loads[2 * ring:2 * ring + 2])))

    return small(kernel, [keep, arrived, *rings], [], [keep.shape])[0]


def scaled_values(product, upper, lower, scale):
    def kernel(product, upper, lower, scale, out):
        half = upper.shape[0]
        for arrived, rows in ((upper, slice(0, half)), (lower, slice(half, 2 * half))):
            out[rows, :] = ((product[rows, :] + arrived[...].astype(F32)) * scale[rows, :]).astype(BF16)

    return small(kernel, [product, upper, lower, scale], [], [product.shape])[0]


def diagonal(width):
    return lax.broadcasted_iota(jnp.int32, (width, width), 0) == lax.broadcasted_iota(jnp.int32, (width, width), 1)


def as_column(row):
    return jnp.sum(jnp.where(diagonal(row.shape[1]), row, 0.0), axis=1, keepdims=True)


def as_row(column):
    return jnp.sum(jnp.where(diagonal(column.shape[0]), column, 0.0), axis=0, keepdims=True)


def scale_kernel(gain, weight, out):
    out[...] = (weight[0].astype(F32) * as_column(gain[...].astype(F32))).astype(BF16)


def scale_weight(gain, weight):
    return pl.pallas_call(scale_kernel, out_shape=jax.ShapeDtypeStruct(weight.shape[1:], BF16), compiler_params=params())(gain, weight)


def finish_kernel(total, gain, weight, grad_weight_in, grad_gain_in, grad_weight, grad_gain):
    half = total.shape[1] // 2
    summed = jnp.concatenate([total[:, :half].astype(F32).T, total[:, half:].astype(F32).T], axis=1)
    grad_weight[0] = grad_weight_in[0] + as_column(gain[...].astype(F32)) * summed
    grad_gain[...] = grad_gain_in[...] + as_row(jnp.sum(weight[0].astype(F32) * summed, axis=1, keepdims=True))


def finish(total, gain, weight, grad_weight_in, grad_gain_in):
    return pl.pallas_call(
        finish_kernel,
        out_shape=[jax.ShapeDtypeStruct(a.shape, F32) for a in (grad_weight_in, grad_gain_in)],
        compiler_params=params(),
    )(total, gain, weight, grad_weight_in, grad_gain_in)


def per_device(hidden, gain, value_weight, cotangent, grad_weight_in, grad_gain_in):
    width = value_weight.shape[1]
    x, z, core = (lax.axis_index(a) for a in ("x", "z", "core"))
    table = jnp.stack(
        [fsdp_index(x ^ flip, (z + off + NZ) % NZ, core) for off in OFFSETS for flip in (0, 1)]
    ).astype(jnp.int32)

    scaled_weight = scale_weight(gain, value_weight)
    layer = [along_blk(scaled_weight, 1, flip) for flip in (0, 1)]

    held, scale, cot_t, *sends = prepare(table, hidden, cotangent, scaled_weight, width)
    visits = [swap_core(send) for send in sends]

    early = [visits[0]] * len(SWAPS)
    sends_1, keeps_1 = gradient(table, held, cot_t, early, cot_t, 0, GROUPS[0], width)
    sends_2, keeps_2 = gradient(table, held, cot_t, visits, sends_1[-1], FIRST, GROUPS[1], width)
    keeps = [*keeps_1, *keeps_2]
    mine = {}

    def send_group(group, index, after):
        first = sum((GROUPS[0] + GROUPS[1])[:index])
        arrived = swap_x(tie([group], after)[0] if after else group)
        for j in range(group.shape[0]):
            mine[OFFSETS[first + j]] = (keeps[first + j], arrived, j)
        return arrived

    arrived = send_group(sends_1[0], 0, [])
    send_group(sends_2[0], 1, [*layer, arrived])

    weights = {0: [(layer[0], width), (layer[1], width)]}
    loads = [begin(layer[ring], mine[4], ring, [keeps_2[-1]]) for ring in (0, 1)]
    for step in (1, 2, 3, 4):
        off = 4 - step
        last = []
        weights[step], weights[-step] = [], []
        for ring in (0, 1):
            up, down = along_z(loads[ring][0], 1), along_z(loads[ring][1], -1)
            if step < 4:
                weights[-step].append((up, width))
                weights[step].append((down, width))
                loads[ring] = advance(up, down, mine[off], mine[-off], ring, width, step, last)
                last = [loads[ring][0]]
                begun = last if ring == 0 else begun
            else:
                weights[step] += [(up, width // 2), (down, width // 2)]
                loads[ring] = [up, down]
        if step < 4:
            send_group(sends_2[step], step + 1, begun)
    total = along_blk(end([*loads[0], *loads[1]], mine[0]), -1, 0)

    near = {off: weights[off] for off in (0, -1, 1, -2, 2)}
    far = {off: weights[off] for off in (-3, 3, 4)}
    products = project(table, held, visits, near, None, [], width)
    product, *products = project(table, held, visits, far, products, [], width)
    values = scaled_values(product, *(swap_core(p) for p in products), scale)

    return values, *finish(total, gain, value_weight, grad_weight_in, grad_gain_in)


def solution(mesh):
    fsdp = ("x", "z", "core")
    return jax.shard_map(
        per_device,
        mesh=Mesh(mesh.devices.reshape(NB, NX, NZ, NC), ("blk", *fsdp)),
        in_specs=(
            P(("blk", *fsdp), None),
            P("blk", fsdp),
            P("blk", fsdp, None),
            P(("blk", *fsdp), None),
            P("blk", fsdp, None),
            P("blk", fsdp),
        ),
        out_specs=(P(("blk", *fsdp), None), P("blk", fsdp, None), P("blk", fsdp)),
        check_vma=False,
    )
```

```python
import functools

import jax
import jax.numpy as jnp
from jax import lax
from jax.experimental import pallas as pl
from jax.experimental.pallas import tpu as pltpu
from jax.sharding import Mesh, PartitionSpec as P

NX, NZ, NC = 2, 8, 2
NB = 8
EPS = 1e-05
BF16 = jnp.bfloat16
F32 = jnp.float32
OFFSETS = (4, 3, -3, 2, -2, 1, -1, 0)
GROUPS = ((1,), (2, 2, 3))
FIRST = sum(GROUPS[0])
SWAPS = (2, 2, 2, 2)
VMEM_LIMIT = 16 * 1024 * 1024
LOAD_LIMIT = 36 * 1024 * 1024


def fsdp_index(x, z, core):
    return (x * NZ + z) * NC + core


def move(value, change):
    pairs = [
        (fsdp_index(x, z, c), fsdp_index(*change(x, z, c)))
        for x in range(NX)
        for z in range(NZ)
        for c in range(NC)
    ]
    return lax.ppermute(value, ("x", "z", "core"), pairs)


def along_z(value, steps):
    return move(value, lambda x, z, c: (x, (z + steps) % NZ, c))


def swap_x(value):
    return move(value, lambda x, z, c: (1 - x, z, c))


def swap_core(value):
    return move(value, lambda x, z, c: (x, z, 1 - c))


def along_blk(value, steps, flip_x, up=0):
    size = NX * NZ * NC
    pairs = [
        (b * size + fsdp_index(x, z, c), ((b + steps) % NB) * size + fsdp_index(x ^ flip_x, (z + up) % NZ, c))
        for b in range(NB)
        for x in range(NX)
        for z in range(NZ)
        for c in range(NC)
    ]
    return lax.ppermute(value, ("blk", "x", "z", "core"), pairs)


def params(limit=VMEM_LIMIT):
    return pltpu.CompilerParams(vmem_limit_bytes=limit)


def cost(flops, size):
    return pl.CostEstimate(flops=flops, bytes_accessed=size, transcendentals=0)


IN_VMEM = pl.BlockSpec(memory_space=pltpu.VMEM)
IN_SMEM = pl.BlockSpec(memory_space=pltpu.SMEM)
ANYWHERE = pl.BlockSpec(memory_space=pl.ANY)
IN_HBM = pl.BlockSpec(memory_space=pltpu.HBM)


def block(ref, index, width):
    return ref[:, pl.ds(pl.multiple_of(index * width, width), width)]


def swapped(visits, index, width):
    for visit, size in zip(visits, SWAPS):
        if index < size:
            return visit[:, 2 * index * width:2 * (index + 1) * width]
        index -= size


def prepare_kernel(width, steps, table, hidden, cot, after, held, scale, cot_t, *rest):
    sends, arrivals = rest[:-1], rest[-1]
    step = hidden.shape[0] // steps
    lanes = 128
    copies = []
    for at in range(steps):
        rows = pl.ds(at * step, step)
        copy = pltpu.make_async_copy(hidden.at[rows, :], held.at[rows, :], arrivals.at[at])
        copy.start()
        copies.append(copy)
    for at in range(steps):
        copies[at].wait()
        rows = slice(at * step, (at + 1) * step)
        total = jnp.zeros((step, lanes), F32)
        for j in range(hidden.shape[1] // lanes):
            part = held[rows, j * lanes:(j + 1) * lanes].astype(F32)
            total += part * part
        inverse = lax.rsqrt(jnp.sum(total, axis=1, keepdims=True) * (1.0 / hidden.shape[1]) + EPS)
        scale[rows, :] = inverse
        columns = (cot[rows, :].astype(F32) * inverse).T.astype(BF16)
        cot_t[:, rows] = columns
        sends[0][:, pl.ds(2 * SWAPS[0] * width + at * step, step)] = columns
        i = 0
        for send, size in zip(sends, SWAPS):
            for j in range(2 * size):
                start = pl.multiple_of((table[i] ^ 1) * width, width)
                send[rows, j * width:(j + 1) * width] = held[rows, pl.ds(start, width)]
                i += 1


def prepare(table, hidden, cot, after, width):
    tokens, features = hidden.shape
    values = cot.shape[1]
    steps = 4
    columns = [2 * size * width for size in SWAPS]
    columns[0] += tokens
    return pl.pallas_call(
        functools.partial(prepare_kernel, width, steps),
        in_specs=[IN_SMEM, IN_HBM, IN_VMEM, ANYWHERE],
        out_specs=[IN_VMEM] * (3 + len(columns)),
        out_shape=[
            jax.ShapeDtypeStruct((tokens, features), BF16),
            jax.ShapeDtypeStruct((tokens, 1), F32),
            jax.ShapeDtypeStruct((values, tokens), BF16),
        ] + [jax.ShapeDtypeStruct((tokens, count), BF16) for count in columns],
        scratch_shapes=[pltpu.SemaphoreType.DMA((steps,))],
        compiler_params=params(LOAD_LIMIT),
        cost_estimate=cost(0, 4 * tokens * features),
    )(table, hidden, cot, after)


def gradient_kernel(base, groups, width, table, hidden, cot_t, *refs):
    visits, outs = refs[:len(SWAPS)], refs[len(SWAPS) + 1:]
    sends = iter(outs[:len(groups)])
    keeps = iter(outs[len(groups):])
    at = base
    for size in groups:
        send = next(sends)
        for j in range(size):
            theirs = swapped(visits, at, width)
            for flip in (1, 0):
                total = jnp.dot(cot_t[...], block(hidden, table[2 * at + flip], width), preferred_element_type=F32)
                total += jnp.dot(
                    visits[0][:, 2 * SWAPS[0] * width:], theirs[:, flip * width:(flip + 1) * width], preferred_element_type=F32
                )
                half = total.shape[0] // 2
                total = jnp.concatenate([total[:half], total[half:]], axis=1).astype(BF16)
                if flip:
                    send[j] = total
                else:
                    next(keeps)[...] = total
            at += 1


def gradient(table, hidden, cot_t, visits, after, base, groups, width):
    tokens = hidden.shape[0]
    values = cot_t.shape[0]
    count = sum(groups)
    outs = pl.pallas_call(
        functools.partial(gradient_kernel, base, groups, width),
        in_specs=[IN_SMEM] + [IN_VMEM] * (2 + len(SWAPS)) + [ANYWHERE],
        out_specs=[IN_VMEM] * (len(groups) + count),
        out_shape=[jax.ShapeDtypeStruct((size, values // 2, 2 * width), BF16) for size in groups]
        + [jax.ShapeDtypeStruct((values // 2, 2 * width), BF16)] * count,
        compiler_params=params(),
        cost_estimate=cost(0, tokens),
    )(table, hidden, cot_t, *visits, after)
    return outs[:len(groups)], outs[len(groups):]


def project_kernel(offsets, rows, more, extra, width, table, hidden, *refs):
    visits, refs = refs[:len(SWAPS)], refs[len(SWAPS):]
    outs = refs[-3:] if more else refs[-2:]
    start = refs[-5 - extra:-3 - extra] if more else None
    refs = iter(refs)
    weights = [[next(refs)[first:first + count] for first, count in group] for group in rows]
    totals = [ref[...] for ref in start] if more else []
    for at in range(0, len(offsets), 2):
        chosen = [OFFSETS.index(off) for off in offsets[at:at + 2]]
        weight = jnp.concatenate([part for group in weights[at:at + 2] for part in group], axis=0)
        own = jnp.concatenate([block(hidden, table[2 * i + flip], width) for i in chosen for flip in (0, 1)], axis=1)
        visitors = jnp.concatenate([swapped(visits, i, width) for i in chosen], axis=1)
        products = [jnp.dot(rows, weight, preferred_element_type=F32) for rows in (own, visitors)]
        totals = [t + p for t, p in zip(totals, products)] if totals else products
    outs[0][...] = totals[0]
    if more:
        half = outs[1].shape[0]
        outs[1][...] = totals[1][:half].astype(BF16)
        outs[2][...] = totals[1][half:].astype(BF16)
    else:
        outs[1][...] = totals[1]


def project(table, hidden, visits, weights, start, after, width):
    tokens = hidden.shape[0]
    arrays = [w for group in weights.values() for w, _, _ in group]
    rows = [[part[1:] for part in group] for group in weights.values()]
    values = arrays[0].shape[-1]
    size = values * sum(count for group in rows for _, count in group)
    more = [] if start is None else list(start)
    whole = jax.ShapeDtypeStruct((tokens, values), F32)
    half = jax.ShapeDtypeStruct((tokens // 2, values), BF16)
    out_shape = [whole, half, half] if more else [whole, whole]
    return pl.pallas_call(
        functools.partial(project_kernel, tuple(weights), rows, bool(more), len(after), width),
        in_specs=[IN_SMEM] + [IN_VMEM] * (1 + len(SWAPS) + len(arrays) + len(more)) + [ANYWHERE] * len(after),
        out_specs=[IN_VMEM] * len(out_shape),
        out_shape=out_shape,
        compiler_params=params(),
        cost_estimate=cost(4 * tokens * size, 0),
    )(table, hidden, *visits, *arrays, *more, *after)


def small(kernel, inputs, after, shapes, dtype=BF16):
    def body(*refs):
        kernel(*refs[:len(inputs)], *refs[len(inputs) + len(after):])

    return pl.pallas_call(
        body,
        in_specs=[IN_VMEM] * len(inputs) + [ANYWHERE] * len(after),
        out_specs=[IN_VMEM] * len(shapes),
        out_shape=[jax.ShapeDtypeStruct(shape, dtype) for shape in shapes],
        compiler_params=params(),
        cost_estimate=cost(0, inputs[0].shape[0]),
    )(*inputs, *after)


def tie(arrays, after):
    count = len(arrays)
    return pl.pallas_call(
        lambda *refs: None,
        in_specs=[ANYWHERE] * (count + len(after)),
        out_specs=[ANYWHERE] * count,
        out_shape=[jax.ShapeDtypeStruct(a.shape, a.dtype) for a in arrays],
        input_output_aliases={i: i for i in range(count)},
        compiler_params=params(),
        cost_estimate=cost(0, 1),
    )(*arrays, *after)


def summed(terms):
    return sum(t.astype(F32) for t in terms).astype(BF16)


def begin(layer, far, ring, after):
    keep, arrived, place = far
    width, values = layer.shape
    part = width // 4

    def kernel(layer, keep, arrived, up, down):
        for i, out in enumerate((up, down)):
            rows = slice((2 * ring + i) * part, (2 * ring + i + 1) * part)
            out[:width] = layer[...]
            out[width:] = summed((keep[rows], arrived[place, rows]))

    return small(kernel, [layer, keep, arrived], after, [(width + part, values)] * 2)


def advance(up, down, above, below, ring, width, step, after):
    values = up.shape[1]
    half = width // 2
    rows = slice(ring * half, (ring + 1) * half)

    def kernel(up, keep_up, arrived_up, down, keep_down, arrived_down, next_up, next_down):
        next_up[:width] = up[:width]
        next_down[:width] = down[:width]
        mine_up = keep_up[rows].astype(F32) + arrived_up[above[2], rows].astype(F32)
        mine_down = keep_down[rows].astype(F32) + arrived_down[below[2], rows].astype(F32)
        came_up, came_down = up[width:].astype(F32), down[width:].astype(F32)
        if step == 1:
            part = half // 2
            mine_up = jnp.concatenate([mine_up[:part] + came_up, mine_up[part:]], axis=0)
            mine_down = jnp.concatenate([mine_down[:part], mine_down[part:] + came_down], axis=0)
        else:
            mine_up += came_up
            mine_down += came_down
        next_up[width:] = mine_up.astype(BF16)
        next_down[width:] = mine_down.astype(BF16)

    return small(kernel, [up, *above[:2], down, *below[:2]], after, [(width + half, values)] * 2)


def nearest(loads, above, below, width, after):
    half = width // 2

    def kernel(*refs):
        for i, place in enumerate((above[2], below[2])):
            keep, arrived = refs[4 + 2 * i:6 + 2 * i]
            sums, layers = refs[8 + i], refs[10 + i]
            for ring in (0, 1):
                load = refs[2 * ring + i]
                rows = slice(ring * half, (ring + 1) * half)
                sums[rows] = summed((keep[rows], arrived[place, rows], load[width:]))
                layers[rows] = load[i * half:(i + 1) * half]

    return small(kernel, [*loads, *above[:2], *below[:2]], after, [above[0].shape] * 4)


def own_part(own):
    keep, arrived, place = own

    def kernel(keep, arrived, out):
        out[...] = summed((keep[...], arrived[place]))

    return small(kernel, [keep, arrived], [], [keep.shape])[0]


def scaled_values(product, upper, lower, scale):
    def kernel(product, upper, lower, scale, out):
        half = upper.shape[0]
        for arrived, rows in ((upper, slice(0, half)), (lower, slice(half, 2 * half))):
            out[rows, :] = ((product[rows, :] + arrived[...].astype(F32)) * scale[rows, :]).astype(BF16)

    return small(kernel, [product, upper, lower, scale], [], [product.shape])[0]


def diagonal(width):
    return lax.broadcasted_iota(jnp.int32, (width, width), 0) == lax.broadcasted_iota(jnp.int32, (width, width), 1)


def as_column(row):
    return jnp.sum(jnp.where(diagonal(row.shape[1]), row, 0.0), axis=1, keepdims=True)


def as_row(column):
    return jnp.sum(jnp.where(diagonal(column.shape[0]), column, 0.0), axis=0, keepdims=True)


def scale_kernel(gain, weight, out):
    out[...] = (weight[0].astype(F32) * as_column(gain[...].astype(F32))).astype(BF16)


def scale_weight(gain, weight):
    return pl.pallas_call(scale_kernel, out_shape=jax.ShapeDtypeStruct(weight.shape[1:], BF16), compiler_params=params())(gain, weight)


def finish_kernel(own, up, down, gain, weight, grad_weight_in, grad_gain_in, grad_weight, grad_gain):
    total = own[...].astype(F32) + up[...].astype(F32) + down[...].astype(F32)
    half = total.shape[1] // 2
    total = jnp.concatenate([total[:, :half].T, total[:, half:].T], axis=1)
    grad_weight[0] = grad_weight_in[0] + as_column(gain[...].astype(F32)) * total
    grad_gain[...] = grad_gain_in[...] + as_row(jnp.sum(weight[0].astype(F32) * total, axis=1, keepdims=True))


def finish(totals, gain, weight, grad_weight_in, grad_gain_in):
    return pl.pallas_call(
        finish_kernel,
        out_shape=[jax.ShapeDtypeStruct(a.shape, F32) for a in (grad_weight_in, grad_gain_in)],
        compiler_params=params(),
    )(*totals, gain, weight, grad_weight_in, grad_gain_in)


def per_device(hidden, gain, value_weight, cotangent, grad_weight_in, grad_gain_in):
    width = value_weight.shape[1]
    x, z, core = (lax.axis_index(a) for a in ("x", "z", "core"))
    table = jnp.stack(
        [fsdp_index(x ^ flip, (z + off + NZ) % NZ, core) for off in OFFSETS for flip in (0, 1)]
    ).astype(jnp.int32)

    scaled_weight = scale_weight(gain, value_weight)
    layer = [along_blk(scaled_weight, 1, flip) for flip in (0, 1)]

    held, scale, cot_t, *sends = prepare(table, hidden, cotangent, scaled_weight, width)
    visits = [swap_core(send) for send in sends]

    early = [visits[0]] * len(SWAPS)
    sends_1, keeps_1 = gradient(table, held, cot_t, early, cot_t, 0, GROUPS[0], width)
    sends_2, keeps_2 = gradient(table, held, cot_t, visits, sends_1[-1], FIRST, GROUPS[1], width)
    keeps = [*keeps_1, *keeps_2]
    mine = {}

    def send_group(group, index, after):
        first = sum((GROUPS[0] + GROUPS[1])[:index])
        arrived = swap_x(tie([group], after)[0] if after else group)
        for j in range(group.shape[0]):
            mine[OFFSETS[first + j]] = (keeps[first + j], arrived, j)
        return arrived

    arrived = send_group(sends_1[0], 0, [])
    send_group(sends_2[0], 1, [*layer, arrived])

    weights = {0: [(layer[0], 0, width), (layer[1], 0, width)]}
    loads = [begin(layer[ring], mine[4], ring, [keeps_2[-1]]) for ring in (0, 1)]
    send_group(sends_2[1], 2, [loads[1][0]])
    for step in (1, 2, 3):
        off = 4 - step
        last = [loads[1][0]] if step == 1 else []
        weights[step], weights[-step] = [], []
        for ring in (0, 1):
            up, down = along_z(loads[ring][0], 1), along_z(loads[ring][1], -1)
            if step == 3 and ring == 0:
                near = {off: weights[off] for off in (0, -1, 1, -2, 2)}
                products = project(table, held, visits, near, None, last, width)
            if step == 3:
                up, down = tie([up, down], [*last, products[0]] if ring else last)
            weights[-step].append((up, 0, width))
            weights[step].append((down, 0, width))
            if step < 3:
                loads[ring] = advance(up, down, mine[off], mine[-off], ring, width, step, last)
            else:
                loads[ring] = [up, down]
            last = [loads[ring][0]]
            if (step, ring) == (1, 0):
                send_group(sends_2[2], 3, last)

    own = along_blk(own_part(mine[0]), -1, 0)
    sum_up, sum_down, layer_up, layer_down = nearest([*loads[0], *loads[1]], mine[1], mine[-1], width, [own])
    totals = [own, along_blk(sum_up, -1, 0, 1), along_blk(sum_down, -1, 0, -1)]
    up, down = along_z(layer_up, 1), along_z(layer_down, -1)
    half = width // 2
    weights[4] = [(far, ring * half, half) for ring in (0, 1) for far in (up, down)]

    far = {off: weights[off] for off in (-3, 3, 4)}
    product, *products = project(table, held, visits, far, products, [], width)
    values = scaled_values(product, *(swap_core(p) for p in products), scale)

    return values, *finish(totals, gain, value_weight, grad_weight_in, grad_gain_in)


def solution(mesh):
    fsdp = ("x", "z", "core")
    return jax.shard_map(
        per_device,
        mesh=Mesh(mesh.devices.reshape(NB, NX, NZ, NC), ("blk", *fsdp)),
        in_specs=(
            P(("blk", *fsdp), None),
            P("blk", fsdp),
            P("blk", fsdp, None),
            P(("blk", *fsdp), None),
            P("blk", fsdp, None),
            P("blk", fsdp),
        ),
        out_specs=(P(("blk", *fsdp), None), P("blk", fsdp, None), P("blk", fsdp)),
        check_vma=False,
    )
```

```python
import functools

import jax
import jax.numpy as jnp
from jax import lax
from jax.experimental import pallas as pl
from jax.experimental.pallas import tpu as pltpu
from jax.sharding import Mesh, PartitionSpec as P

NX, NZ, NC = 2, 8, 2
NB = 8
EPS = 1e-05
BF16 = jnp.bfloat16
F32 = jnp.float32
OFFSETS = (4, 3, -3, 2, -2, 1, -1, 0)
GROUPS = ((1,), (2, 2, 3))
FIRST = sum(GROUPS[0])
SENT_AFTER = ((1, 0), (1, 1), (2, 0))
SWAPS = (2, 2, 2, 2)
PIECES = 4
VMEM_LIMIT = 16 * 1024 * 1024
LOAD_LIMIT = 36 * 1024 * 1024


def fsdp_index(x, z, core):
    return (x * NZ + z) * NC + core


def move(value, change):
    pairs = [
        (fsdp_index(x, z, c), fsdp_index(*change(x, z, c)))
        for x in range(NX)
        for z in range(NZ)
        for c in range(NC)
    ]
    return lax.ppermute(value, ("x", "z", "core"), pairs)


def along_z(value, steps):
    return move(value, lambda x, z, c: (x, (z + steps) % NZ, c))


def swap_x(value):
    return move(value, lambda x, z, c: (1 - x, z, c))


def swap_core(value):
    return move(value, lambda x, z, c: (x, z, 1 - c))


def along_blk(value, steps, flip_x, up=0):
    size = NX * NZ * NC
    pairs = [
        (b * size + fsdp_index(x, z, c), ((b + steps) % NB) * size + fsdp_index(x ^ flip_x, (z + up) % NZ, c))
        for b in range(NB)
        for x in range(NX)
        for z in range(NZ)
        for c in range(NC)
    ]
    return lax.ppermute(value, ("blk", "x", "z", "core"), pairs)


def params(limit=VMEM_LIMIT):
    return pltpu.CompilerParams(vmem_limit_bytes=limit)


def cost(flops, size):
    return pl.CostEstimate(flops=flops, bytes_accessed=size, transcendentals=0)


IN_VMEM = pl.BlockSpec(memory_space=pltpu.VMEM)
IN_SMEM = pl.BlockSpec(memory_space=pltpu.SMEM)
ANYWHERE = pl.BlockSpec(memory_space=pl.ANY)
IN_HBM = pl.BlockSpec(memory_space=pltpu.HBM)


def block(ref, index, width):
    return ref[:, pl.ds(pl.multiple_of(index * width, width), width)]


def swapped(visits, index, width):
    for visit, size in zip(visits, SWAPS):
        if index < size:
            return visit[:, 2 * index * width:2 * (index + 1) * width]
        index -= size


def prepare_kernel(width, steps, table, hidden, cot, after, held, scale, cot_t, *rest):
    sends, arrivals = rest[:-1], rest[-1]
    step = hidden.shape[0] // steps
    lanes = 128
    copies = []
    for at in range(steps):
        rows = pl.ds(at * step, step)
        copy = pltpu.make_async_copy(hidden.at[rows, :], held.at[rows, :], arrivals.at[at])
        copy.start()
        copies.append(copy)
    for at in range(steps):
        copies[at].wait()
        rows = slice(at * step, (at + 1) * step)
        total = jnp.zeros((step, lanes), F32)
        for j in range(hidden.shape[1] // lanes):
            part = held[rows, j * lanes:(j + 1) * lanes].astype(F32)
            total += part * part
        inverse = lax.rsqrt(jnp.sum(total, axis=1, keepdims=True) * (1.0 / hidden.shape[1]) + EPS)
        scale[rows, :] = inverse
        columns = (cot[rows, :].astype(F32) * inverse).T.astype(BF16)
        cot_t[:, rows] = columns
        sends[0][:, pl.ds(2 * SWAPS[0] * width + at * step, step)] = columns
        i = 0
        for send, size in zip(sends, SWAPS):
            for j in range(2 * size):
                start = pl.multiple_of((table[i] ^ 1) * width, width)
                send[rows, j * width:(j + 1) * width] = held[rows, pl.ds(start, width)]
                i += 1


def prepare(table, hidden, cot, after, width):
    tokens, features = hidden.shape
    values = cot.shape[1]
    steps = 4
    columns = [2 * size * width for size in SWAPS]
    columns[0] += tokens
    return pl.pallas_call(
        functools.partial(prepare_kernel, width, steps),
        in_specs=[IN_SMEM, IN_HBM, IN_VMEM, ANYWHERE],
        out_specs=[IN_VMEM] * (3 + len(columns)),
        out_shape=[
            jax.ShapeDtypeStruct((tokens, features), BF16),
            jax.ShapeDtypeStruct((tokens, 1), F32),
            jax.ShapeDtypeStruct((values, tokens), BF16),
        ] + [jax.ShapeDtypeStruct((tokens, count), BF16) for count in columns],
        scratch_shapes=[pltpu.SemaphoreType.DMA((steps,))],
        compiler_params=params(LOAD_LIMIT),
        cost_estimate=cost(0, 4 * tokens * features),
    )(table, hidden, cot, after)


def gradient_kernel(base, groups, width, table, hidden, cot_t, *refs):
    visits, outs = refs[:len(SWAPS)], refs[len(SWAPS) + 1:]
    sends = iter(outs[:len(groups)])
    keeps = iter(outs[len(groups):])
    at = base
    for size in groups:
        send = next(sends)
        for j in range(size):
            theirs = swapped(visits, at, width)
            for flip in (1, 0):
                total = jnp.dot(cot_t[...], block(hidden, table[2 * at + flip], width), preferred_element_type=F32)
                total += jnp.dot(
                    visits[0][:, 2 * SWAPS[0] * width:], theirs[:, flip * width:(flip + 1) * width], preferred_element_type=F32
                )
                half = total.shape[0] // 2
                total = jnp.concatenate([total[:half], total[half:]], axis=1).astype(BF16)
                if flip:
                    send[j] = total
                else:
                    next(keeps)[...] = total
            at += 1


def gradient(table, hidden, cot_t, visits, after, base, groups, width):
    tokens = hidden.shape[0]
    values = cot_t.shape[0]
    count = sum(groups)
    outs = pl.pallas_call(
        functools.partial(gradient_kernel, base, groups, width),
        in_specs=[IN_SMEM] + [IN_VMEM] * (2 + len(SWAPS)) + [ANYWHERE],
        out_specs=[IN_VMEM] * (len(groups) + count),
        out_shape=[jax.ShapeDtypeStruct((size, values // 2, 2 * width), BF16) for size in groups]
        + [jax.ShapeDtypeStruct((values // 2, 2 * width), BF16)] * count,
        compiler_params=params(),
        cost_estimate=cost(0, tokens),
    )(table, hidden, cot_t, *visits, after)
    return outs[:len(groups)], outs[len(groups):]


def project_kernel(offsets, rows, more, final, extra, width, table, hidden, *refs):
    visits, refs = refs[:len(SWAPS)], refs[len(SWAPS):]
    count = 1 + PIECES if final else 2
    outs = refs[-count:]
    start = refs[-count - extra - 2:-count - extra]
    refs = iter(refs)
    weights = [[next(refs)[first:first + count] for first, count in group] for group in rows]
    totals = [ref[...] for ref in start] if more else []
    for at in range(0, len(offsets), 2):
        chosen = [OFFSETS.index(off) for off in offsets[at:at + 2]]
        weight = jnp.concatenate([part for group in weights[at:at + 2] for part in group], axis=0)
        own = jnp.concatenate([block(hidden, table[2 * i + flip], width) for i in chosen for flip in (0, 1)], axis=1)
        visitors = jnp.concatenate([swapped(visits, i, width) for i in chosen], axis=1)
        products = [jnp.dot(rows, weight, preferred_element_type=F32) for rows in (own, visitors)]
        totals = [t + p for t, p in zip(totals, products)] if totals else products
    outs[0][...] = totals[0]
    if final:
        part = outs[1].shape[0]
        for i, out in enumerate(outs[1:]):
            out[...] = totals[1][i * part:(i + 1) * part].astype(BF16)
    else:
        outs[1][...] = totals[1]


def project(table, hidden, visits, weights, start, after, width, final=False):
    tokens = hidden.shape[0]
    arrays = [w for group in weights.values() for w, _, _ in group]
    rows = [[part[1:] for part in group] for group in weights.values()]
    values = arrays[0].shape[-1]
    size = values * sum(count for group in rows for _, count in group)
    more = [] if start is None else list(start)
    whole = jax.ShapeDtypeStruct((tokens, values), F32)
    part = jax.ShapeDtypeStruct((tokens // PIECES, values), BF16)
    out_shape = [whole, *[part] * PIECES] if final else [whole, whole]
    return pl.pallas_call(
        functools.partial(project_kernel, tuple(weights), rows, bool(more), final, len(after), width),
        in_specs=[IN_SMEM] + [IN_VMEM] * (1 + len(SWAPS) + len(arrays) + len(more)) + [ANYWHERE] * len(after),
        out_specs=[IN_VMEM] * len(out_shape),
        out_shape=out_shape,
        compiler_params=params(),
        cost_estimate=cost(4 * tokens * size, 0),
    )(table, hidden, *visits, *arrays, *more, *after)


def small(kernel, inputs, after, shapes, dtype=BF16):
    def body(*refs):
        kernel(*refs[:len(inputs)], *refs[len(inputs) + len(after):])

    return pl.pallas_call(
        body,
        in_specs=[IN_VMEM] * len(inputs) + [ANYWHERE] * len(after),
        out_specs=[IN_VMEM] * len(shapes),
        out_shape=[jax.ShapeDtypeStruct(shape, dtype) for shape in shapes],
        compiler_params=params(),
        cost_estimate=cost(0, inputs[0].shape[0]),
    )(*inputs, *after)


def tie(arrays, after):
    count = len(arrays)
    return pl.pallas_call(
        lambda *refs: None,
        in_specs=[ANYWHERE] * (count + len(after)),
        out_specs=[ANYWHERE] * count,
        out_shape=[jax.ShapeDtypeStruct(a.shape, a.dtype) for a in arrays],
        input_output_aliases={i: i for i in range(count)},
        compiler_params=params(),
        cost_estimate=cost(0, 1),
    )(*arrays, *after)


def summed(terms):
    return sum(t.astype(F32) for t in terms).astype(BF16)


def begin(layers, far, ring, after):
    keep, arrived, place = far
    width, values = layers[0].shape
    part = width // 4

    def kernel(layer_up, layer_down, keep, arrived, up, down):
        for i, (layer, out) in enumerate(((layer_up, up), (layer_down, down))):
            rows = slice((2 * ring + i) * part, (2 * ring + i + 1) * part)
            out[:width] = layer[...]
            out[width:] = summed((keep[rows], arrived[place, rows]))

    return small(kernel, [*layers, keep, arrived], after, [(width + part, values)] * 2)


def advance(up, down, above, below, ring, width, step, after):
    values = up.shape[1]
    half = width // 2
    rows = slice(ring * half, (ring + 1) * half)
    layer_rows = width if step == 1 else half

    def kernel(up, keep_up, arrived_up, down, keep_down, arrived_down, next_up, next_down):
        next_up[:layer_rows] = up[:layer_rows]
        next_down[:layer_rows] = down[width - layer_rows:width]
        mine_up = keep_up[rows].astype(F32) + arrived_up[above[2], rows].astype(F32)
        mine_down = keep_down[rows].astype(F32) + arrived_down[below[2], rows].astype(F32)
        came_up, came_down = up[width:].astype(F32), down[width:].astype(F32)
        if step == 1:
            part = half // 2
            mine_up = jnp.concatenate([mine_up[:part] + came_up, mine_up[part:]], axis=0)
            mine_down = jnp.concatenate([mine_down[:part], mine_down[part:] + came_down], axis=0)
        else:
            mine_up += came_up
            mine_down += came_down
        next_up[layer_rows:] = mine_up.astype(BF16)
        next_down[layer_rows:] = mine_down.astype(BF16)

    return small(kernel, [up, *above[:2], down, *below[:2]], after, [(layer_rows + half, values)] * 2)


def nearest(loads, above, below, after):
    half = above[0].shape[0] // 2

    def kernel(*refs):
        for i, place in enumerate((above[2], below[2])):
            keep, arrived = refs[4 + 2 * i:6 + 2 * i]
            for ring in (0, 1):
                rows = slice(ring * half, (ring + 1) * half)
                refs[8 + i][rows] = summed((keep[rows], arrived[place, rows], refs[2 * ring + i][half:]))

    return small(kernel, [*loads, *above[:2], *below[:2]], after, [above[0].shape] * 2)


def own_part(own):
    keep, arrived, place = own

    def kernel(keep, arrived, out):
        out[...] = summed((keep[...], arrived[place]))

    return small(kernel, [keep, arrived], [], [keep.shape])[0]


def scaled_values(product, pieces, scale):
    def kernel(product, *refs):
        arrived, scale, out = refs[:PIECES], refs[-2], refs[-1]
        part = arrived[0].shape[0]
        for i, piece in enumerate(arrived):
            rows = slice(i * part, (i + 1) * part)
            out[rows, :] = ((product[rows, :] + piece[...].astype(F32)) * scale[rows, :]).astype(BF16)

    return small(kernel, [product, *pieces, scale], [], [product.shape])[0]


def diagonal(width):
    return lax.broadcasted_iota(jnp.int32, (width, width), 0) == lax.broadcasted_iota(jnp.int32, (width, width), 1)


def as_column(row):
    return jnp.sum(jnp.where(diagonal(row.shape[1]), row, 0.0), axis=1, keepdims=True)


def as_row(column):
    return jnp.sum(jnp.where(diagonal(column.shape[0]), column, 0.0), axis=0, keepdims=True)


def scale_kernel(gain, weight, out):
    out[...] = (weight[0].astype(F32) * as_column(gain[...].astype(F32))).astype(BF16)


def scale_weight(gain, weight):
    return pl.pallas_call(scale_kernel, out_shape=jax.ShapeDtypeStruct(weight.shape[1:], BF16), compiler_params=params())(gain, weight)


def finish_kernel(own, up, down, gain, weight, grad_weight_in, grad_gain_in, grad_weight, grad_gain):
    total = own[...].astype(F32) + up[...].astype(F32) + down[...].astype(F32)
    half = total.shape[1] // 2
    total = jnp.concatenate([total[:, :half].T, total[:, half:].T], axis=1)
    grad_weight[0] = grad_weight_in[0] + as_column(gain[...].astype(F32)) * total
    grad_gain[...] = grad_gain_in[...] + as_row(jnp.sum(weight[0].astype(F32) * total, axis=1, keepdims=True))


def finish(totals, gain, weight, grad_weight_in, grad_gain_in):
    return pl.pallas_call(
        finish_kernel,
        out_shape=[jax.ShapeDtypeStruct(a.shape, F32) for a in (grad_weight_in, grad_gain_in)],
        compiler_params=params(),
    )(*totals, gain, weight, grad_weight_in, grad_gain_in)


def per_device(hidden, gain, value_weight, cotangent, grad_weight_in, grad_gain_in):
    width = value_weight.shape[1]
    x, z, core = (lax.axis_index(a) for a in ("x", "z", "core"))
    table = jnp.stack(
        [fsdp_index(x ^ flip, (z + off + NZ) % NZ, core) for off in OFFSETS for flip in (0, 1)]
    ).astype(jnp.int32)

    scaled_weight = scale_weight(gain, value_weight)
    layer = [along_blk(scaled_weight, 1, flip) for flip in (0, 1)]

    held, scale, cot_t, *sends = prepare(table, hidden, cotangent, scaled_weight, width)
    visits = [swap_core(send) for send in sends]

    early = [visits[0]] * len(SWAPS)
    sends_1, keeps_1 = gradient(table, held, cot_t, early, cot_t, 0, GROUPS[0], width)
    sends_2, keeps_2 = gradient(table, held, cot_t, visits, sends_1[-1], FIRST, GROUPS[1], width)
    keeps = [*keeps_1, *keeps_2]
    mine = {}

    def send_group(group, index, after):
        first = sum((GROUPS[0] + GROUPS[1])[:index])
        arrived = swap_x(tie([group], after)[0] if after else group)
        for j in range(group.shape[0]):
            mine[OFFSETS[first + j]] = (keeps[first + j], arrived, j)
        return arrived

    layer = tie(layer, [keeps_2[-1]])
    send_group(sends_1[0], 0, layer)

    weights = {0: [(layer[0], 0, width), (layer[1], 0, width)]}
    loads = [(layer[ring], layer[ring]) for ring in (0, 1)]
    for step in (1, 2, 3, 4):
        weights[step], weights[-step] = [], []
        moved = [(along_z(load[0], 1), along_z(load[1], -1)) for load in loads]
        last = [*moved[1]] if step == 1 else []
        for ring in (0, 1):
            up, down = moved[ring]
            if step == 4:
                if ring == 1:
                    middle = {off: weights[off] for off in (-3, 3)}
                    products = project(table, held, visits, middle, products, last, width)
                    last = [*last, products[0]]
                up, down = tie([up, down], last)
                weights[step] += [(up, 0, width // 2), (down, 0, width // 2)]
                loads[ring] = [up, down]
            else:
                weights[-step].append((up, 0, width))
                weights[step].append((down, 0, width))
                if (step, ring) == (3, 1):
                    near = {off: weights[off] for off in (0, -1, 1, -2, 2)}
                    products = project(table, held, visits, near, None, [], width)
                    last = [*last, products[0]]
                if step == 1:
                    loads[ring] = begin((up, down), mine[4], ring, last)
                else:
                    loads[ring] = advance(up, down, mine[5 - step], mine[step - 5], ring, width, step - 1, last)
            last = [loads[ring][0]]
            if (step, ring) in SENT_AFTER:
                group = SENT_AFTER.index((step, ring))
                send_group(sends_2[group], group + 1, last)

    own = along_blk(own_part(mine[0]), -1, 0)
    sum_up, sum_down = nearest([*loads[0], *loads[1]], mine[1], mine[-1], [own])
    totals = [own, along_blk(sum_up, -1, 0, 1), along_blk(sum_down, -1, 0, -1)]
    product, *products = project(table, held, visits, {4: weights[4]}, products, [sum_up], width, final=True)
    values = scaled_values(product, [swap_core(p) for p in products], scale)

    return values, *finish(totals, gain, value_weight, grad_weight_in, grad_gain_in)


def solution(mesh):
    fsdp = ("x", "z", "core")
    return jax.shard_map(
        per_device,
        mesh=Mesh(mesh.devices.reshape(NB, NX, NZ, NC), ("blk", *fsdp)),
        in_specs=(
            P(("blk", *fsdp), None),
            P("blk", fsdp),
            P("blk", fsdp, None),
            P(("blk", *fsdp), None),
            P("blk", fsdp, None),
            P("blk", fsdp),
        ),
        out_specs=(P(("blk", *fsdp), None), P("blk", fsdp, None), P("blk", fsdp)),
        check_vma=False,
    )
```

```python
import functools

import jax
import jax.numpy as jnp
from jax import lax
from jax.experimental import pallas as pl
from jax.experimental.pallas import tpu as pltpu
from jax.sharding import Mesh, PartitionSpec as P

NX, NZ, NC = 2, 8, 2
NB = 8
EPS = 1e-05
BF16 = jnp.bfloat16
F32 = jnp.float32
OFFSETS = (4, 3, -3, 2, -2, 1, -1, 0)
GROUPS = ((1,), (2, 2, 3))
FIRST = sum(GROUPS[0])
SWAPS = (2, 2, 2, 2)
VMEM_LIMIT = 16 * 1024 * 1024
LOAD_LIMIT = 36 * 1024 * 1024


def fsdp_index(x, z, core):
    return (x * NZ + z) * NC + core


def move(value, change):
    pairs = [
        (fsdp_index(x, z, c), fsdp_index(*change(x, z, c)))
        for x in range(NX)
        for z in range(NZ)
        for c in range(NC)
    ]
    return lax.ppermute(value, ("x", "z", "core"), pairs)


def along_z(value, steps):
    return move(value, lambda x, z, c: (x, (z + steps) % NZ, c))


def swap_x(value):
    return move(value, lambda x, z, c: (1 - x, z, c))


def swap_core(value):
    return move(value, lambda x, z, c: (x, z, 1 - c))


def along_blk(value, steps, flip_x, up=0):
    size = NX * NZ * NC
    pairs = [
        (b * size + fsdp_index(x, z, c), ((b + steps) % NB) * size + fsdp_index(x ^ flip_x, (z + up) % NZ, c))
        for b in range(NB)
        for x in range(NX)
        for z in range(NZ)
        for c in range(NC)
    ]
    return lax.ppermute(value, ("blk", "x", "z", "core"), pairs)


def params(limit=VMEM_LIMIT):
    return pltpu.CompilerParams(vmem_limit_bytes=limit)


def cost(flops, size):
    return pl.CostEstimate(flops=flops, bytes_accessed=size, transcendentals=0)


IN_VMEM = pl.BlockSpec(memory_space=pltpu.VMEM)
IN_SMEM = pl.BlockSpec(memory_space=pltpu.SMEM)
ANYWHERE = pl.BlockSpec(memory_space=pl.ANY)
IN_HBM = pl.BlockSpec(memory_space=pltpu.HBM)


def block(ref, index, width):
    return ref[:, pl.ds(pl.multiple_of(index * width, width), width)]


def swapped(visits, index, width):
    for visit, size in zip(visits, SWAPS):
        if index < size:
            return visit[:, 2 * index * width:2 * (index + 1) * width]
        index -= size


def prepare_kernel(width, steps, table, hidden, cot, held, scale, cot_t, *rest):
    sends, arrivals = rest[:-1], rest[-1]
    step = hidden.shape[0] // steps
    lanes = 128
    copies = []
    for at in range(steps):
        rows = pl.ds(at * step, step)
        copy = pltpu.make_async_copy(hidden.at[rows, :], held.at[rows, :], arrivals.at[at])
        copy.start()
        copies.append(copy)
    for at in range(steps):
        copies[at].wait()
        rows = slice(at * step, (at + 1) * step)
        total = jnp.zeros((step, lanes), F32)
        for j in range(hidden.shape[1] // lanes):
            part = held[rows, j * lanes:(j + 1) * lanes].astype(F32)
            total += part * part
        inverse = lax.rsqrt(jnp.sum(total, axis=1, keepdims=True) * (1.0 / hidden.shape[1]) + EPS)
        scale[rows, :] = inverse
        columns = (cot[rows, :].astype(F32) * inverse).T.astype(BF16)
        cot_t[:, rows] = columns
        sends[0][:, pl.ds(2 * SWAPS[0] * width + at * step, step)] = columns
        i = 0
        for send, size in zip(sends, SWAPS):
            for j in range(2 * size):
                start = pl.multiple_of((table[i] ^ 1) * width, width)
                send[rows, j * width:(j + 1) * width] = held[rows, pl.ds(start, width)]
                i += 1


def prepare(table, hidden, cot, width):
    tokens, features = hidden.shape
    values = cot.shape[1]
    steps = 4
    columns = [2 * size * width for size in SWAPS]
    columns[0] += tokens
    return pl.pallas_call(
        functools.partial(prepare_kernel, width, steps),
        in_specs=[IN_SMEM, IN_HBM, IN_VMEM],
        out_specs=[IN_VMEM] * (3 + len(columns)),
        out_shape=[
            jax.ShapeDtypeStruct((tokens, features), BF16),
            jax.ShapeDtypeStruct((tokens, 1), F32),
            jax.ShapeDtypeStruct((values, tokens), BF16),
        ] + [jax.ShapeDtypeStruct((tokens, count), BF16) for count in columns],
        scratch_shapes=[pltpu.SemaphoreType.DMA((steps,))],
        compiler_params=params(LOAD_LIMIT),
        cost_estimate=cost(0, 4 * tokens * features),
    )(table, hidden, cot)


def gradient_kernel(base, groups, width, table, hidden, cot_t, *refs):
    visits, outs = refs[:len(SWAPS)], refs[len(SWAPS) + 1:]
    sends = iter(outs[:len(groups)])
    keeps = iter(outs[len(groups):])
    at = base
    for size in groups:
        send = next(sends)
        for j in range(size):
            theirs = swapped(visits, at, width)
            for flip in (1, 0):
                total = jnp.dot(cot_t[...], block(hidden, table[2 * at + flip], width), preferred_element_type=F32)
                total += jnp.dot(
                    visits[0][:, 2 * SWAPS[0] * width:], theirs[:, flip * width:(flip + 1) * width], preferred_element_type=F32
                )
                half = total.shape[0] // 2
                total = jnp.concatenate([total[:half], total[half:]], axis=1).astype(BF16)
                if flip:
                    send[j] = total
                else:
                    next(keeps)[...] = total
            at += 1


def gradient(table, hidden, cot_t, visits, after, base, groups, width):
    tokens = hidden.shape[0]
    values = cot_t.shape[0]
    count = sum(groups)
    outs = pl.pallas_call(
        functools.partial(gradient_kernel, base, groups, width),
        in_specs=[IN_SMEM] + [IN_VMEM] * (2 + len(SWAPS)) + [ANYWHERE],
        out_specs=[IN_VMEM] * (len(groups) + count),
        out_shape=[jax.ShapeDtypeStruct((size, values // 2, 2 * width), BF16) for size in groups]
        + [jax.ShapeDtypeStruct((values // 2, 2 * width), BF16)] * count,
        compiler_params=params(),
        cost_estimate=cost(0, tokens),
    )(table, hidden, cot_t, *visits, after)
    return outs[:len(groups)], outs[len(groups):]


def project_kernel(offsets, rows, more, final, extra, width, table, hidden, *refs):
    visits, refs = refs[:len(SWAPS)], refs[len(SWAPS):]
    count = 3 if final else 2
    outs = refs[-count:]
    start = refs[-count - extra - 2:-count - extra]
    refs = iter(refs)
    weights = [[next(refs)[first:first + count] for first, count in group] for group in rows]
    totals = [ref[...] for ref in start] if more else []
    for at in range(0, len(offsets), 2):
        chosen = [OFFSETS.index(off) for off in offsets[at:at + 2]]
        weight = jnp.concatenate([part for group in weights[at:at + 2] for part in group], axis=0)
        own = jnp.concatenate([block(hidden, table[2 * i + flip], width) for i in chosen for flip in (0, 1)], axis=1)
        visitors = jnp.concatenate([swapped(visits, i, width) for i in chosen], axis=1)
        products = [jnp.dot(rows, weight, preferred_element_type=F32) for rows in (own, visitors)]
        totals = [t + p for t, p in zip(totals, products)] if totals else products
    outs[0][...] = totals[0]
    if final:
        half = outs[1].shape[0]
        outs[1][...] = totals[1][:half].astype(BF16)
        outs[2][...] = totals[1][half:].astype(BF16)
    else:
        outs[1][...] = totals[1]


def project(table, hidden, visits, weights, start, after, width, final=False):
    tokens = hidden.shape[0]
    arrays = [w for group in weights.values() for w, _, _ in group]
    rows = [[part[1:] for part in group] for group in weights.values()]
    values = arrays[0].shape[-1]
    size = values * sum(count for group in rows for _, count in group)
    more = [] if start is None else list(start)
    whole = jax.ShapeDtypeStruct((tokens, values), F32)
    half = jax.ShapeDtypeStruct((tokens // 2, values), BF16)
    out_shape = [whole, half, half] if final else [whole, whole]
    return pl.pallas_call(
        functools.partial(project_kernel, tuple(weights), rows, bool(more), final, len(after), width),
        in_specs=[IN_SMEM] + [IN_VMEM] * (1 + len(SWAPS) + len(arrays) + len(more)) + [ANYWHERE] * len(after),
        out_specs=[IN_VMEM] * len(out_shape),
        out_shape=out_shape,
        compiler_params=params(),
        cost_estimate=cost(4 * tokens * size, 0),
    )(table, hidden, *visits, *arrays, *more, *after)


def small(kernel, inputs, after, shapes, dtype=BF16):
    def body(*refs):
        kernel(*refs[:len(inputs)], *refs[len(inputs) + len(after):])

    return pl.pallas_call(
        body,
        in_specs=[IN_VMEM] * len(inputs) + [ANYWHERE] * len(after),
        out_specs=[IN_VMEM] * len(shapes),
        out_shape=[jax.ShapeDtypeStruct(shape, dtype) for shape in shapes],
        compiler_params=params(),
        cost_estimate=cost(0, inputs[0].shape[0]),
    )(*inputs, *after)


def tie(arrays, after):
    count = len(arrays)
    return pl.pallas_call(
        lambda *refs: None,
        in_specs=[ANYWHERE] * (count + len(after)),
        out_specs=[ANYWHERE] * count,
        out_shape=[jax.ShapeDtypeStruct(a.shape, a.dtype) for a in arrays],
        input_output_aliases={i: i for i in range(count)},
        compiler_params=params(),
        cost_estimate=cost(0, 1),
    )(*arrays, *after)


def summed(terms):
    return sum(t.astype(F32) for t in terms).astype(BF16)


def begin(layer, far, ring, after):
    keep, arrived, place = far
    width, values = layer.shape
    part = width // 4

    def kernel(layer, keep, arrived, up, down):
        for i, out in enumerate((up, down)):
            rows = slice((2 * ring + i) * part, (2 * ring + i + 1) * part)
            out[:width] = layer[...]
            out[width:] = summed((keep[rows], arrived[place, rows]))

    return small(kernel, [layer, keep, arrived], after, [(width + part, values)] * 2)


def advance(up, down, above, below, ring, width, step, after):
    values = up.shape[1]
    half = width // 2
    rows = slice(ring * half, (ring + 1) * half)

    def kernel(up, keep_up, arrived_up, down, keep_down, arrived_down, next_up, next_down):
        next_up[:width] = up[:width]
        next_down[:width] = down[:width]
        mine_up = keep_up[rows].astype(F32) + arrived_up[above[2], rows].astype(F32)
        mine_down = keep_down[rows].astype(F32) + arrived_down[below[2], rows].astype(F32)
        came_up, came_down = up[width:].astype(F32), down[width:].astype(F32)
        if step == 1:
            part = half // 2
            mine_up = jnp.concatenate([mine_up[:part] + came_up, mine_up[part:]], axis=0)
            mine_down = jnp.concatenate([mine_down[:part], mine_down[part:] + came_down], axis=0)
        else:
            mine_up += came_up
            mine_down += came_down
        next_up[width:] = mine_up.astype(BF16)
        next_down[width:] = mine_down.astype(BF16)

    return small(kernel, [up, *above[:2], down, *below[:2]], after, [(width + half, values)] * 2)


def nearest(loads, above, below, width, after):
    half = width // 2

    def kernel(*refs):
        for i, place in enumerate((above[2], below[2])):
            keep, arrived = refs[4 + 2 * i:6 + 2 * i]
            sums, layers = refs[8 + i], refs[10 + i]
            for ring in (0, 1):
                load = refs[2 * ring + i]
                rows = slice(ring * half, (ring + 1) * half)
                sums[rows] = summed((keep[rows], arrived[place, rows], load[width:]))
                layers[rows] = load[i * half:(i + 1) * half]

    return small(kernel, [*loads, *above[:2], *below[:2]], after, [above[0].shape] * 4)


def own_part(own):
    keep, arrived, place = own

    def kernel(keep, arrived, out):
        out[...] = summed((keep[...], arrived[place]))

    return small(kernel, [keep, arrived], [], [keep.shape])[0]


def scaled_values(product, upper, lower, scale):
    def kernel(product, upper, lower, scale, out):
        half = upper.shape[0]
        for arrived, rows in ((upper, slice(0, half)), (lower, slice(half, 2 * half))):
            out[rows, :] = ((product[rows, :] + arrived[...].astype(F32)) * scale[rows, :]).astype(BF16)

    return small(kernel, [product, upper, lower, scale], [], [product.shape])[0]


def diagonal(width):
    return lax.broadcasted_iota(jnp.int32, (width, width), 0) == lax.broadcasted_iota(jnp.int32, (width, width), 1)


def as_column(row):
    return jnp.sum(jnp.where(diagonal(row.shape[1]), row, 0.0), axis=1, keepdims=True)


def as_row(column):
    return jnp.sum(jnp.where(diagonal(column.shape[0]), column, 0.0), axis=0, keepdims=True)


def scale_kernel(gain, weight, out):
    out[...] = (weight[0].astype(F32) * as_column(gain[...].astype(F32))).astype(BF16)


def scale_weight(gain, weight):
    return pl.pallas_call(scale_kernel, out_shape=jax.ShapeDtypeStruct(weight.shape[1:], BF16), compiler_params=params())(gain, weight)


def finish_kernel(own, up, down, gain, weight, grad_weight_in, grad_gain_in, grad_weight, grad_gain):
    total = own[...].astype(F32) + up[...].astype(F32) + down[...].astype(F32)
    half = total.shape[1] // 2
    total = jnp.concatenate([total[:, :half].T, total[:, half:].T], axis=1)
    grad_weight[0] = grad_weight_in[0] + as_column(gain[...].astype(F32)) * total
    grad_gain[...] = grad_gain_in[...] + as_row(jnp.sum(weight[0].astype(F32) * total, axis=1, keepdims=True))


def finish(totals, gain, weight, grad_weight_in, grad_gain_in):
    return pl.pallas_call(
        finish_kernel,
        out_shape=[jax.ShapeDtypeStruct(a.shape, F32) for a in (grad_weight_in, grad_gain_in)],
        compiler_params=params(),
    )(*totals, gain, weight, grad_weight_in, grad_gain_in)


def per_device(hidden, gain, value_weight, cotangent, grad_weight_in, grad_gain_in):
    width = value_weight.shape[1]
    x, z, core = (lax.axis_index(a) for a in ("x", "z", "core"))
    table = jnp.stack(
        [fsdp_index(x ^ flip, (z + off + NZ) % NZ, core) for off in OFFSETS for flip in (0, 1)]
    ).astype(jnp.int32)

    scaled_weight = scale_weight(gain, value_weight)
    layer = [along_blk(scaled_weight, 1, flip) for flip in (0, 1)]

    held, scale, cot_t, *sends = prepare(table, hidden, cotangent, width)
    visits = [swap_core(send) for send in sends]

    early = [visits[0]] * len(SWAPS)
    sends_1, keeps_1 = gradient(table, held, cot_t, early, cot_t, 0, GROUPS[0], width)
    sends_2, keeps_2 = gradient(table, held, cot_t, visits, sends_1[-1], FIRST, GROUPS[1], width)
    keeps = [*keeps_1, *keeps_2]
    mine = {}

    def send_group(group, index, after):
        first = sum((GROUPS[0] + GROUPS[1])[:index])
        arrived = swap_x(tie([group], after)[0] if after else group)
        for j in range(group.shape[0]):
            mine[OFFSETS[first + j]] = (keeps[first + j], arrived, j)
        return arrived

    arrived = send_group(sends_1[0], 0, [])
    send_group(sends_2[0], 1, [*layer, arrived])

    weights = {0: [(layer[0], 0, width), (layer[1], 0, width)]}
    loads = [begin(layer[ring], mine[4], ring, [keeps_2[-1]]) for ring in (0, 1)]
    send_group(sends_2[1], 2, [loads[1][0]])
    for step in (1, 2, 3):
        off = 4 - step
        last = [loads[1][0]] if step == 1 else []
        weights[step], weights[-step] = [], []
        for ring in (0, 1):
            up, down = along_z(loads[ring][0], 1), along_z(loads[ring][1], -1)
            if step == 3 and ring == 0:
                near = {off: weights[off] for off in (0, -1, 1, -2, 2)}
                products = project(table, held, visits, near, None, last, width)
            if step == 3:
                up, down = tie([up, down], [*last, products[0]] if ring else last)
            weights[-step].append((up, 0, width))
            weights[step].append((down, 0, width))
            if step < 3:
                loads[ring] = advance(up, down, mine[off], mine[-off], ring, width, step, last)
            else:
                loads[ring] = [up, down]
            last = [loads[ring][0]]
            if (step, ring) == (1, 0):
                send_group(sends_2[2], 3, last)

    own = along_blk(own_part(mine[0]), -1, 0)
    sum_up, sum_down, layer_up, layer_down = nearest([*loads[0], *loads[1]], mine[1], mine[-1], width, [own])
    totals = [own, along_blk(sum_up, -1, 0, 1), along_blk(sum_down, -1, 0, -1)]
    up, down = along_z(layer_up, 1), along_z(layer_down, -1)
    half = width // 2
    weights[4] = [(far, ring * half, half) for ring in (0, 1) for far in (up, down)]

    middle = {off: weights[off] for off in (-3, 3)}
    products = project(table, held, visits, middle, products, [sum_up], width)
    product, *products = project(table, held, visits, {4: weights[4]}, products, [], width, final=True)
    values = scaled_values(product, *(swap_core(p) for p in products), scale)

    return values, *finish(totals, gain, value_weight, grad_weight_in, grad_gain_in)


def solution(mesh):
    fsdp = ("x", "z", "core")
    return jax.shard_map(
        per_device,
        mesh=Mesh(mesh.devices.reshape(NB, NX, NZ, NC), ("blk", *fsdp)),
        in_specs=(
            P(("blk", *fsdp), None),
            P("blk", fsdp),
            P("blk", fsdp, None),
            P(("blk", *fsdp), None),
            P("blk", fsdp, None),
            P("blk", fsdp),
        ),
        out_specs=(P(("blk", *fsdp), None), P("blk", fsdp, None), P("blk", fsdp)),
        check_vma=False,
    )
```

```python
import functools

import jax
import jax.numpy as jnp
from jax import lax
from jax.experimental import pallas as pl
from jax.experimental.pallas import tpu as pltpu
from jax.sharding import Mesh, PartitionSpec as P

NX, NZ, NC = 2, 8, 2
NB = 8
EPS = 1e-05
BF16 = jnp.bfloat16
F32 = jnp.float32
OFFSETS = (4, 3, -3, 2, -2, 0, 1, -1)
GROUPS = ((1,), (2, 2, 1, 2))
FIRST = sum(GROUPS[0])
SWAPS = (2, 2, 2, 2)
VMEM_LIMIT = 16 * 1024 * 1024
LOAD_LIMIT = 36 * 1024 * 1024


def fsdp_index(x, z, core):
    return (x * NZ + z) * NC + core


def move(value, change):
    pairs = [
        (fsdp_index(x, z, c), fsdp_index(*change(x, z, c)))
        for x in range(NX)
        for z in range(NZ)
        for c in range(NC)
    ]
    return lax.ppermute(value, ("x", "z", "core"), pairs)


def along_z(value, steps):
    return move(value, lambda x, z, c: (x, (z + steps) % NZ, c))


def swap_x(value):
    return move(value, lambda x, z, c: (1 - x, z, c))


def swap_core(value):
    return move(value, lambda x, z, c: (x, z, 1 - c))


def along_blk(value, steps, flip_x, up=0):
    size = NX * NZ * NC
    pairs = [
        (b * size + fsdp_index(x, z, c), ((b + steps) % NB) * size + fsdp_index(x ^ flip_x, (z + up) % NZ, c))
        for b in range(NB)
        for x in range(NX)
        for z in range(NZ)
        for c in range(NC)
    ]
    return lax.ppermute(value, ("blk", "x", "z", "core"), pairs)


def params(limit=VMEM_LIMIT):
    return pltpu.CompilerParams(vmem_limit_bytes=limit)


def cost(flops, size):
    return pl.CostEstimate(flops=flops, bytes_accessed=size, transcendentals=0)


IN_VMEM = pl.BlockSpec(memory_space=pltpu.VMEM)
IN_SMEM = pl.BlockSpec(memory_space=pltpu.SMEM)
ANYWHERE = pl.BlockSpec(memory_space=pl.ANY)
IN_HBM = pl.BlockSpec(memory_space=pltpu.HBM)


def block(ref, index, width):
    return ref[:, pl.ds(pl.multiple_of(index * width, width), width)]


def swapped(visits, index, width):
    for visit, size in zip(visits, SWAPS):
        if index < size:
            return visit[:, 2 * index * width:2 * (index + 1) * width]
        index -= size


def prepare_kernel(width, steps, table, hidden, cot, held, scale, cot_t, *rest):
    sends, arrivals = rest[:-1], rest[-1]
    step = hidden.shape[0] // steps
    lanes = 128
    copies = []
    for at in range(steps):
        rows = pl.ds(at * step, step)
        copy = pltpu.make_async_copy(hidden.at[rows, :], held.at[rows, :], arrivals.at[at])
        copy.start()
        copies.append(copy)
    for at in range(steps):
        copies[at].wait()
        rows = slice(at * step, (at + 1) * step)
        total = jnp.zeros((step, lanes), F32)
        for j in range(hidden.shape[1] // lanes):
            part = held[rows, j * lanes:(j + 1) * lanes].astype(F32)
            total += part * part
        inverse = lax.rsqrt(jnp.sum(total, axis=1, keepdims=True) * (1.0 / hidden.shape[1]) + EPS)
        scale[rows, :] = inverse
        columns = (cot[rows, :].astype(F32) * inverse).T.astype(BF16)
        cot_t[:, rows] = columns
        sends[0][:, pl.ds(2 * SWAPS[0] * width + at * step, step)] = columns
        i = 0
        for send, size in zip(sends, SWAPS):
            for j in range(2 * size):
                start = pl.multiple_of((table[i] ^ 1) * width, width)
                send[rows, j * width:(j + 1) * width] = held[rows, pl.ds(start, width)]
                i += 1


def prepare(table, hidden, cot, width):
    tokens, features = hidden.shape
    values = cot.shape[1]
    steps = 4
    columns = [2 * size * width for size in SWAPS]
    columns[0] += tokens
    return pl.pallas_call(
        functools.partial(prepare_kernel, width, steps),
        in_specs=[IN_SMEM, IN_HBM, IN_VMEM],
        out_specs=[IN_VMEM] * (3 + len(columns)),
        out_shape=[
            jax.ShapeDtypeStruct((tokens, features), BF16),
            jax.ShapeDtypeStruct((tokens, 1), F32),
            jax.ShapeDtypeStruct((values, tokens), BF16),
        ] + [jax.ShapeDtypeStruct((tokens, count), BF16) for count in columns],
        scratch_shapes=[pltpu.SemaphoreType.DMA((steps,))],
        compiler_params=params(LOAD_LIMIT),
        cost_estimate=cost(0, 4 * tokens * features),
    )(table, hidden, cot)


def gradient_kernel(base, groups, width, table, hidden, cot_t, *refs):
    visits, outs = refs[:len(SWAPS)], refs[len(SWAPS) + 1:]
    sends = iter(outs[:len(groups)])
    keeps = iter(outs[len(groups):])
    at = base
    for size in groups:
        send = next(sends)
        for j in range(size):
            theirs = swapped(visits, at, width)
            for flip in (1, 0):
                total = jnp.dot(cot_t[...], block(hidden, table[2 * at + flip], width), preferred_element_type=F32)
                total += jnp.dot(
                    visits[0][:, 2 * SWAPS[0] * width:], theirs[:, flip * width:(flip + 1) * width], preferred_element_type=F32
                )
                half = total.shape[0] // 2
                total = jnp.concatenate([total[:half], total[half:]], axis=1).astype(BF16)
                if flip:
                    send[j] = total
                else:
                    next(keeps)[...] = total
            at += 1


def gradient(table, hidden, cot_t, visits, after, base, groups, width):
    tokens = hidden.shape[0]
    values = cot_t.shape[0]
    count = sum(groups)
    outs = pl.pallas_call(
        functools.partial(gradient_kernel, base, groups, width),
        in_specs=[IN_SMEM] + [IN_VMEM] * (2 + len(SWAPS)) + [ANYWHERE],
        out_specs=[IN_VMEM] * (len(groups) + count),
        out_shape=[jax.ShapeDtypeStruct((size, values // 2, 2 * width), BF16) for size in groups]
        + [jax.ShapeDtypeStruct((values // 2, 2 * width), BF16)] * count,
        compiler_params=params(),
        cost_estimate=cost(0, tokens),
    )(table, hidden, cot_t, *visits, after)
    return outs[:len(groups)], outs[len(groups):]


def project_kernel(offsets, rows, more, final, extra, width, table, hidden, *refs):
    visits, refs = refs[:len(SWAPS)], refs[len(SWAPS):]
    count = 3 if final else 2
    outs = refs[-count:]
    start = refs[-count - extra - 2:-count - extra]
    refs = iter(refs)
    weights = [[next(refs)[first:first + count] for first, count in group] for group in rows]
    totals = [ref[...] for ref in start] if more else []
    for at in range(0, len(offsets), 2):
        chosen = [OFFSETS.index(off) for off in offsets[at:at + 2]]
        weight = jnp.concatenate([part for group in weights[at:at + 2] for part in group], axis=0)
        own = jnp.concatenate([block(hidden, table[2 * i + flip], width) for i in chosen for flip in (0, 1)], axis=1)
        visitors = jnp.concatenate([swapped(visits, i, width) for i in chosen], axis=1)
        products = [jnp.dot(rows, weight, preferred_element_type=F32) for rows in (own, visitors)]
        totals = [t + p for t, p in zip(totals, products)] if totals else products
    outs[0][...] = totals[0]
    if final:
        half = outs[1].shape[0]
        outs[1][...] = totals[1][:half].astype(BF16)
        outs[2][...] = totals[1][half:].astype(BF16)
    else:
        outs[1][...] = totals[1]


def project(table, hidden, visits, weights, start, after, width, final=False):
    tokens = hidden.shape[0]
    arrays = [w for group in weights.values() for w, _, _ in group]
    rows = [[part[1:] for part in group] for group in weights.values()]
    values = arrays[0].shape[-1]
    size = values * sum(count for group in rows for _, count in group)
    more = [] if start is None else list(start)
    whole = jax.ShapeDtypeStruct((tokens, values), F32)
    half = jax.ShapeDtypeStruct((tokens // 2, values), BF16)
    out_shape = [whole, half, half] if final else [whole, whole]
    return pl.pallas_call(
        functools.partial(project_kernel, tuple(weights), rows, bool(more), final, len(after), width),
        in_specs=[IN_SMEM] + [IN_VMEM] * (1 + len(SWAPS) + len(arrays) + len(more)) + [ANYWHERE] * len(after),
        out_specs=[IN_VMEM] * len(out_shape),
        out_shape=out_shape,
        compiler_params=params(),
        cost_estimate=cost(4 * tokens * size, 0),
    )(table, hidden, *visits, *arrays, *more, *after)


def small(kernel, inputs, after, shapes, dtype=BF16):
    def body(*refs):
        kernel(*refs[:len(inputs)], *refs[len(inputs) + len(after):])

    return pl.pallas_call(
        body,
        in_specs=[IN_VMEM] * len(inputs) + [ANYWHERE] * len(after),
        out_specs=[IN_VMEM] * len(shapes),
        out_shape=[jax.ShapeDtypeStruct(shape, dtype) for shape in shapes],
        compiler_params=params(),
        cost_estimate=cost(0, inputs[0].shape[0]),
    )(*inputs, *after)


def tie(arrays, after):
    count = len(arrays)
    return pl.pallas_call(
        lambda *refs: None,
        in_specs=[ANYWHERE] * (count + len(after)),
        out_specs=[ANYWHERE] * count,
        out_shape=[jax.ShapeDtypeStruct(a.shape, a.dtype) for a in arrays],
        input_output_aliases={i: i for i in range(count)},
        compiler_params=params(),
        cost_estimate=cost(0, 1),
    )(*arrays, *after)


def summed(terms):
    return sum(t.astype(F32) for t in terms).astype(BF16)


def begin(layer, far, ring, after):
    keep, arrived, place = far
    width, values = layer.shape
    part = width // 4

    def kernel(layer, keep, arrived, up, down):
        for i, out in enumerate((up, down)):
            rows = slice((2 * ring + i) * part, (2 * ring + i + 1) * part)
            out[:width] = layer[...]
            out[width:] = summed((keep[rows], arrived[place, rows]))

    return small(kernel, [layer, keep, arrived], after, [(width + part, values)] * 2)


def advance(up, down, above, below, ring, width, step, after):
    values = up.shape[1]
    half = width // 2
    rows = slice(ring * half, (ring + 1) * half)

    def kernel(up, keep_up, arrived_up, down, keep_down, arrived_down, next_up, next_down):
        next_up[:width] = up[:width]
        next_down[:width] = down[:width]
        mine_up = keep_up[rows].astype(F32) + arrived_up[above[2], rows].astype(F32)
        mine_down = keep_down[rows].astype(F32) + arrived_down[below[2], rows].astype(F32)
        came_up, came_down = up[width:].astype(F32), down[width:].astype(F32)
        if step == 1:
            part = half // 2
            mine_up = jnp.concatenate([mine_up[:part] + came_up, mine_up[part:]], axis=0)
            mine_down = jnp.concatenate([mine_down[:part], mine_down[part:] + came_down], axis=0)
        else:
            mine_up += came_up
            mine_down += came_down
        next_up[width:] = mine_up.astype(BF16)
        next_down[width:] = mine_down.astype(BF16)

    return small(kernel, [up, *above[:2], down, *below[:2]], after, [(width + half, values)] * 2)


def nearest(loads, above, below, width, after):
    half = width // 2

    def kernel(*refs):
        for i, place in enumerate((above[2], below[2])):
            keep, arrived = refs[4 + 2 * i:6 + 2 * i]
            sums, layers = refs[8 + i], refs[10 + i]
            for ring in (0, 1):
                load = refs[2 * ring + i]
                rows = slice(ring * half, (ring + 1) * half)
                sums[rows] = summed((keep[rows], arrived[place, rows], load[width:]))
                layers[rows] = load[i * half:(i + 1) * half]

    return small(kernel, [*loads, *above[:2], *below[:2]], after, [above[0].shape] * 4)


def own_part(own):
    keep, arrived, place = own

    def kernel(keep, arrived, out):
        out[...] = summed((keep[...], arrived[place]))

    return small(kernel, [keep, arrived], [], [keep.shape])[0]


def scaled_values(product, upper, lower, scale):
    def kernel(product, upper, lower, scale, out):
        half = upper.shape[0]
        for arrived, rows in ((upper, slice(0, half)), (lower, slice(half, 2 * half))):
            out[rows, :] = ((product[rows, :] + arrived[...].astype(F32)) * scale[rows, :]).astype(BF16)

    return small(kernel, [product, upper, lower, scale], [], [product.shape])[0]


def diagonal(width):
    return lax.broadcasted_iota(jnp.int32, (width, width), 0) == lax.broadcasted_iota(jnp.int32, (width, width), 1)


def as_column(row):
    return jnp.sum(jnp.where(diagonal(row.shape[1]), row, 0.0), axis=1, keepdims=True)


def as_row(column):
    return jnp.sum(jnp.where(diagonal(column.shape[0]), column, 0.0), axis=0, keepdims=True)


def scale_kernel(gain, weight, out):
    out[...] = (weight[0].astype(F32) * as_column(gain[...].astype(F32))).astype(BF16)


def scale_weight(gain, weight):
    return pl.pallas_call(scale_kernel, out_shape=jax.ShapeDtypeStruct(weight.shape[1:], BF16), compiler_params=params())(gain, weight)


def finish_kernel(own, up, down, gain, weight, grad_weight_in, grad_gain_in, grad_weight, grad_gain):
    total = own[...].astype(F32) + up[...].astype(F32) + down[...].astype(F32)
    half = total.shape[1] // 2
    total = jnp.concatenate([total[:, :half].T, total[:, half:].T], axis=1)
    grad_weight[0] = grad_weight_in[0] + as_column(gain[...].astype(F32)) * total
    grad_gain[...] = grad_gain_in[...] + as_row(jnp.sum(weight[0].astype(F32) * total, axis=1, keepdims=True))


def finish(totals, gain, weight, grad_weight_in, grad_gain_in):
    return pl.pallas_call(
        finish_kernel,
        out_shape=[jax.ShapeDtypeStruct(a.shape, F32) for a in (grad_weight_in, grad_gain_in)],
        compiler_params=params(),
    )(*totals, gain, weight, grad_weight_in, grad_gain_in)


def per_device(hidden, gain, value_weight, cotangent, grad_weight_in, grad_gain_in):
    width = value_weight.shape[1]
    x, z, core = (lax.axis_index(a) for a in ("x", "z", "core"))
    table = jnp.stack(
        [fsdp_index(x ^ flip, (z + off + NZ) % NZ, core) for off in OFFSETS for flip in (0, 1)]
    ).astype(jnp.int32)

    scaled_weight = scale_weight(gain, value_weight)
    layer = [along_blk(scaled_weight, 1, flip) for flip in (0, 1)]

    held, scale, cot_t, *sends = prepare(table, hidden, cotangent, width)
    visits = [swap_core(send) for send in sends]

    early = [visits[0]] * len(SWAPS)
    sends_1, keeps_1 = gradient(table, held, cot_t, early, cot_t, 0, GROUPS[0], width)
    sends_2, keeps_2 = gradient(table, held, cot_t, visits, sends_1[-1], FIRST, GROUPS[1], width)
    keeps = [*keeps_1, *keeps_2]
    mine = {}

    def send_group(group, index, after):
        first = sum((GROUPS[0] + GROUPS[1])[:index])
        arrived = swap_x(tie([group], after)[0] if after else group)
        for j in range(group.shape[0]):
            mine[OFFSETS[first + j]] = (keeps[first + j], arrived, j)
        return arrived

    arrived = send_group(sends_1[0], 0, [])
    send_group(sends_2[0], 1, [*layer, arrived])

    weights = {0: [(layer[0], 0, width), (layer[1], 0, width)]}
    loads = [begin(layer[ring], mine[4], ring, [keeps_2[-1]]) for ring in (0, 1)]
    send_group(sends_2[1], 2, [loads[1][0]])
    for step in (1, 2, 3):
        off = 4 - step
        last = [loads[1][0]] if step == 1 else []
        weights[step], weights[-step] = [], []
        for ring in (0, 1):
            up, down = along_z(loads[ring][0], 1), along_z(loads[ring][1], -1)
            if step == 3 and ring == 0:
                near = {off: weights[off] for off in (0, -1, 1, -2, 2)}
                products = project(table, held, visits, near, None, last, width)
            if step == 3:
                up, down = tie([up, down], [*last, products[0]] if ring else last)
            weights[-step].append((up, 0, width))
            weights[step].append((down, 0, width))
            if step < 3:
                loads[ring] = advance(up, down, mine[off], mine[-off], ring, width, step, last)
            else:
                loads[ring] = [up, down]
            last = [loads[ring][0]]
            if step == 1:
                send_group(sends_2[2 + ring], 3 + ring, last)

    own = along_blk(own_part(mine[0]), -1, 0)
    sum_up, sum_down, layer_up, layer_down = nearest([*loads[0], *loads[1]], mine[1], mine[-1], width, [own])
    totals = [own, along_blk(sum_up, -1, 0, 1), along_blk(sum_down, -1, 0, -1)]
    up, down = along_z(layer_up, 1), along_z(layer_down, -1)
    half = width // 2
    weights[4] = [(far, ring * half, half) for ring in (0, 1) for far in (up, down)]

    middle = {off: weights[off] for off in (-3, 3)}
    products = project(table, held, visits, middle, products, [sum_up], width)
    product, *products = project(table, held, visits, {4: weights[4]}, products, [], width, final=True)
    values = scaled_values(product, *(swap_core(p) for p in products), scale)

    return values, *finish(totals, gain, value_weight, grad_weight_in, grad_gain_in)


def solution(mesh):
    fsdp = ("x", "z", "core")
    return jax.shard_map(
        per_device,
        mesh=Mesh(mesh.devices.reshape(NB, NX, NZ, NC), ("blk", *fsdp)),
        in_specs=(
            P(("blk", *fsdp), None),
            P("blk", fsdp),
            P("blk", fsdp, None),
            P(("blk", *fsdp), None),
            P("blk", fsdp, None),
            P("blk", fsdp),
        ),
        out_specs=(P(("blk", *fsdp), None), P("blk", fsdp, None), P("blk", fsdp)),
        check_vma=False,
    )
```
